128 devices in a mesh: grp: 8 (over x, core), blk: 16 (over y, z).
Axes of the slice: x: 4, y: 4, z: 4, core: 2. Of those that a mesh axis runs over, the one named last changes fastest.
Arguments:
- stamps: float32 [128, 128, 64, 128], P(('grp', 'blk')), may hold values from -1 to 1
- stamp_target: int32 [128, 128, 128], P(('grp', 'blk')), may hold values from 0 to 4095
- pair_counts: int32 [128, 128], P(('grp', 'blk')), may hold values from 0 to 128, as said below
- conductance: float32 [8, 32768], P(None, ('grp', 'blk')), may hold values from 4 to 12
- block_cols: int32 [16, 32768], P(None, ('grp', 'blk')), may hold values from 0 to 32767, as said below
- newton_residual: float32 [8, 32768], P(None, ('grp', 'blk')), may hold values from -30 to 30
Outputs:
- update: float32 [8, 32768], P(None, ('grp', 'blk'))
- jacobian_blocks: float32 [16, 8, 8, 32768], P(None, None, None, ('grp', 'blk'))
- preconditioned_rhs: float32 [8, 32768], P(None, ('grp', 'blk'))
The draws below stay inside these ranges and needn't reach their ends.
Inputs may be any that keep to these rules, and one draw needn't show every extreme that they name: `stamp_target`: A stamp's target is its block slot times 256 plus its block row local to the owner. `pair_counts`: every device sends exactly 128 live blocks to itself and exactly 128 to the next device in the order of grp+blk (the last device to the first), and at most 32 to every other owner; one owner drawn from the seed receives exactly 32 from every device other than itself and the device before it. `block_cols`: slot 0 of block row n names n itself; slots 1 to 7 name rows of the same group of 4096 rows as n; over the 256 block rows of one device, the slots from 8 on name rows owned by each device exactly 16 times.
All inputs are finite; a program needn't handle non-finite values.
Results may differ from the reference program's by a relative error of at most 0.0003.
Values sent between devices are 32-bit elements; how exact they have to be, the bound alone decides.
A program may use at most 128 MiB of HBM per device.

```python
import math
import jax
import jax.numpy as jnp
from jax import lax

NBR = 256
CAP = 128
K = 16
KRYLOV = 5
SWEEPS = 2
LOW = 32
NB = 32768
GROUP_ROWS = 4096
DEVICES = 128


def draw_pair_counts(key, part):
    key_hot, key_cold, key_warm, key_full = jax.random.split(jax.random.fold_in(key, 11), 4)
    hot = jax.random.randint(key_hot, (1, DEVICES), 0, 4) == 0
    cold_counts = jax.random.randint(key_cold, (DEVICES, DEVICES), LOW // 4, LOW // 2 + 1)
    warm_counts = jax.random.randint(key_warm, (DEVICES, DEVICES), LOW // 2, LOW + 1)
    counts = jnp.where(hot, warm_counts, cold_counts)
    full_owner = jax.random.randint(key_full, (), 0, DEVICES)
    col_ids = jnp.arange(DEVICES)[None, :]
    row_ids = jnp.arange(DEVICES)[:, None]
    counts = jnp.where(col_ids == full_owner, LOW, counts)
    paired = (row_ids == col_ids) | (col_ids == (row_ids + 1) % DEVICES)
    counts = jnp.where(paired, CAP, counts)
    return counts.astype(jnp.int32)


def shuffle_one(one_key):
    return jax.random.permutation(one_key, (K - K // 2) * NBR)


def draw_block_cols(key, part):
    key_near, key_owner, key_row = jax.random.split(jax.random.fold_in(key, 23), 3)
    row_ids = jnp.arange(NB, dtype=jnp.int32)
    group_start = row_ids // GROUP_ROWS * GROUP_ROWS
    near_cols = group_start[None, :] + jax.random.randint(key_near, (K // 2 - 1, NB), 0, GROUP_ROWS)
    far_slots = K - K // 2
    owner_keys = jax.random.split(key_owner, DEVICES)
    shuffled = jax.vmap(shuffle_one)(owner_keys)
    far_owner = shuffled % DEVICES
    far_local = jax.random.randint(key_row, (DEVICES, far_slots * NBR), 0, NBR)
    far_cols = (far_owner * NBR + far_local).reshape(DEVICES, far_slots, NBR)
    far_cols = far_cols.transpose(1, 0, 2).reshape(far_slots, NB)
    return jnp.concatenate([row_ids[None, :], near_cols, far_cols.astype(jnp.int32)], axis=0).astype(jnp.int32)


def touch_ends(values, own_key, least, largest):
    shape = values.shape
    place = [jax.random.randint(jax.random.fold_in(own_key, axis), (), 0, shape[axis]) for axis in range(len(shape))]
    values = values.at[tuple(place)].set(least)
    longest = shape.index(max(shape))
    place[longest] = (place[longest] + 1) % shape[longest]
    return values.at[tuple(place)].set(largest)


def block_scale(key, extent, pieces, smallest, largest):
    level = 1.0
    for axis_at, blocks in pieces:
        draws = jax.random.uniform(jax.random.fold_in(jax.random.fold_in(key, 6), axis_at), (blocks,), jnp.float32, smallest / len(pieces), largest / len(pieces))
        level = level * jnp.repeat(jnp.exp(draws), extent[axis_at] // blocks).reshape((-1,) + (1,) * (len(extent) - 1 - axis_at))
    return level


def bell_draw(stream_key, shape, deviation, reach, cuts=(), held_as=jnp.bfloat16):
    level = block_scale(stream_key, shape, cuts, -0.22, 0.18) if cuts else 1.0
    array = jax.random.normal(stream_key, shape, jnp.float32) * deviation * level
    return jnp.minimum(jnp.maximum(array, -reach), reach).astype(held_as)


def setup_inputs(seed: int = 0) -> dict:
    streams_of = jax.random.split(jax.random.key(seed), 7)
    stamps = jnp.clip(jax.random.uniform(streams_of[0], (DEVICES, DEVICES, 64, CAP), jnp.float32, -1.0, 1.0) * block_scale(streams_of[0], (DEVICES, DEVICES, 64, CAP), ((0, 128),), -0.4, 0.0), -1.0, 1.0)
    stamp_target = touch_ends(jax.random.randint(streams_of[1], (DEVICES, DEVICES, CAP), 0, K * NBR), jax.random.fold_in(streams_of[1], 1), 0, (K * NBR) - 1).astype(jnp.int32)
    pair_counts = draw_pair_counts(jax.random.fold_in(streams_of[6], 71), 0)
    conductance = jnp.clip(jnp.exp(math.log(12.0) - 1.0986123 * jax.random.uniform(streams_of[3], (8, NB), jnp.float32) ** block_scale(streams_of[3], (8, NB), ((1, 128),), -0.2, 0.2)), 4.0, 12.0)
    block_cols = draw_block_cols(jax.random.fold_in(streams_of[6], 71), 0)
    newton_residual = bell_draw(streams_of[5], (8, NB), 5.0, 30.0, ((1, 128),), jnp.float32)
    return {"stamps": stamps, "stamp_target": stamp_target, "pair_counts": pair_counts, "conductance": conductance, "block_cols": block_cols, "newton_residual": newton_residual}


EPS = 1e-06

def invert_blocks(diag):
    size = diag.shape[0]
    eye_mat = jnp.eye(size, dtype=jnp.float32)[:, :, None]
    inverse = eye_mat * jnp.ones_like(diag[:1])
    work = diag
    for pivot_row in range(size):
        scale = 1.0 / work[pivot_row, pivot_row]
        top_work = work[pivot_row] * scale
        top_inverse = inverse[pivot_row] * scale
        factor = work[:, pivot_row]
        work = work - factor[:, None, :] * top_work[None]
        inverse = inverse - factor[:, None, :] * top_inverse[None]
        work = work.at[pivot_row].set(top_work)
        inverse = inverse.at[pivot_row].set(top_inverse)
    return inverse

def solve_small(matrix, rhs_vector):
    count = matrix.shape[0]
    work, vector = (matrix, rhs_vector)
    for pivot_row in range(count):
        scale = 1.0 / work[pivot_row, pivot_row]
        top_work = work[pivot_row] * scale
        top_rhs = vector[pivot_row] * scale
        factor = work[:, pivot_row]
        work = work - factor[:, None] * top_work[None, :]
        vector = vector - factor * top_rhs
        work = work.at[pivot_row].set(top_work)
        vector = vector.at[pivot_row].set(top_rhs)
    return vector

def block_apply(inverse, vector):
    return jnp.einsum('abn,bn->an', inverse, vector, precision=lax.Precision.HIGHEST)

def couple(jacobian, picked):
    return jnp.einsum('kabn,bkn->an', jacobian, picked, precision=lax.Precision.HIGHEST)

def reference(stamps, stamp_target, pair_counts, conductance, block_cols, newton_residual):
    slot_ids = jnp.arange(CAP, dtype=jnp.int32)
    owners = jnp.arange(DEVICES, dtype=jnp.int32)

    def add_source(summed, source):
        values, targets, counts = source
        live = slot_ids[None, :] < counts[:, None]
        values = jnp.where(live[:, None, :], values, 0.0)
        where_to = targets // NBR * NB + owners[:, None] * NBR + targets % NBR
        flat = values.transpose(1, 0, 2).reshape(64, DEVICES * CAP)
        return (summed.at[:, where_to.reshape(-1)].add(flat), None)
    summed, _ = lax.scan(add_source, jnp.zeros((64, K * NB), jnp.float32), (stamps, stamp_target, pair_counts))
    jacobian = summed.reshape(8, 8, K, NB).transpose(2, 0, 1, 3)
    identity = jnp.eye(8, dtype=jnp.float32)
    jacobian = jacobian.at[0].add(identity[:, :, None] * conductance[:, None, :])
    inverse = invert_blocks(jacobian[0])
    row_ids = jnp.arange(NB, dtype=jnp.int32)
    near = (block_cols // GROUP_ROWS == (row_ids // GROUP_ROWS)[None, :]) & (jnp.arange(K, dtype=jnp.int32)[:, None] >= 1)

    def precondition(vector):
        result = block_apply(inverse, vector)
        for sweep_index in range(SWEEPS):
            picked = jnp.where(near[None], result[:, block_cols], 0.0)
            result = block_apply(inverse, vector - couple(jacobian, picked))
        return result

    def operate(vector):
        return couple(jacobian, vector[:, block_cols])
    rhs_field = -newton_residual
    beta = jnp.sqrt(jnp.sum(rhs_field * rhs_field) + EPS)
    basis = [rhs_field / beta]
    search = []
    hess = jnp.zeros((KRYLOV + 1, KRYLOV), jnp.float32)
    for krylov_step in range(KRYLOV):
        direction = precondition(basis[krylov_step])
        search.append(direction)
        image = operate(direction)
        projections = jnp.stack([jnp.sum(basis_vec * image) for basis_vec in basis])
        for index_i, basis_vec in enumerate(basis):
            image = image - projections[index_i] * basis_vec
        length = jnp.sqrt(jnp.sum(image * image) + EPS)
        hess = hess.at[:krylov_step + 1, krylov_step].set(projections)
        hess = hess.at[krylov_step + 1, krylov_step].set(length)
        if krylov_step + 1 < KRYLOV:
            basis.append(image / length)
    normal = jnp.dot(hess.T, hess, precision=lax.Precision.HIGHEST)
    coef = solve_small(normal, beta * hess[0])
    update = coef[0] * search[0]
    for index_j in range(1, KRYLOV):
        update = update + coef[index_j] * search[index_j]
    return (update, jacobian, beta * search[0])
```

```python
import functools
import jax
import jax.numpy as jnp
from jax import lax
from jax.experimental import pallas as pl
from jax.experimental.pallas import tpu as pltpu
from jax.sharding import PartitionSpec as P

K = 16
KRYLOV = 5
NBR = 256
NGRP = 8
NBLK = 16
DEVICES = 128
LANES = 128
EPS = 1e-06
MESH = pl.DeviceIdType.MESH
AXES = ("grp", "blk")


def bf(x):
    return x.astype(jnp.float32).astype(jnp.bfloat16)


def iota(shape, dim):
    return lax.broadcasted_iota(jnp.int32, shape, dim)


def lane_pick(table, index):
    return jnp.take_along_axis(table, index, axis=1, mode="promise_in_bounds")


def fold_rows(parts):
    row = iota(parts[0].shape, 0)
    step = 1
    while len(parts) > 1:
        even = (row & step) == 0
        merged = []
        for first, second in zip(parts[0::2], parts[1::2]):
            kept = jnp.where(even, first, second)
            moved = jnp.where(even, second, first)
            merged.append(kept + pltpu.roll(moved, step, 0))
        parts = merged
        step *= 2
    return parts[0]


def block_mul(blocks, vector):
    return fold_rows([blocks[a] * vector for a in range(8)])


def small_solve(gram, scales):
    inv = [1.0 / s for s in scales] + [1.0]
    sc = list(scales) + [1.0]
    n = KRYLOV + 1
    g = [[None] * n for _ in range(n)]
    for l in range(n):
        for m in range(l + 1):
            val = gram[l][m] * sc[l] * sc[m]
            g[l][m] = val
            g[m][l] = val
    beta = jnp.sqrt(gram[0][0] + EPS)
    basis = [[inv[0] / beta]]
    hess = []
    for j in range(KRYLOV):
        b = basis[j]
        w = [None] * (j + 2)
        for l in range(j + 1):
            w[l] = b[l] if w[l] is None else w[l] + b[l]
            w[l + 1] = b[l] * inv[l + 1]
        gw = []
        for l in range(j + 2):
            t = g[l][0] * w[0]
            for m in range(1, j + 2):
                t = t + g[l][m] * w[m]
            gw.append(t)
        column = []
        for i in range(j + 1):
            t = basis[i][0] * gw[0]
            for l in range(1, i + 1):
                t = t + basis[i][l] * gw[l]
            column.append(t)
        for i in range(j + 1):
            for l in range(i + 1):
                w[l] = w[l] - column[i] * basis[i][l]
        sq = None
        for l in range(j + 2):
            t = g[l][0] * w[0]
            for m in range(1, j + 2):
                t = t + g[l][m] * w[m]
            sq = t * w[l] if sq is None else sq + t * w[l]
        length = jnp.sqrt(jnp.maximum(sq, 0.0) + EPS)
        column.append(length)
        hess.append(column)
        scale = 1.0 / length
        basis.append([x * scale for x in w])
    work = [[None] * KRYLOV for _ in range(KRYLOV)]
    for p in range(KRYLOV):
        for q in range(p + 1):
            t = hess[p][0] * hess[q][0]
            for i in range(1, q + 2):
                t = t + hess[p][i] * hess[q][i]
            work[p][q] = t
            work[q][p] = t
    vec = [beta * hess[p][0] for p in range(KRYLOV)]
    for p in range(KRYLOV):
        scale = 1.0 / work[p][p]
        top = [x * scale for x in work[p]]
        tv = vec[p] * scale
        for q in range(KRYLOV):
            if q == p:
                continue
            f = work[q][p]
            work[q] = [x - f * y for x, y in zip(work[q], top)]
            vec[q] = vec[q] - f * tv
        work[p] = top
        vec[p] = tv
    out = []
    for l in range(KRYLOV):
        t = None
        for j in range(l, KRYLOV):
            x = vec[j] * basis[j][l]
            t = x if t is None else t + x
        out.append(t * sc[l])
    return out


def krylov_kernel(jac, dinv, res, cols, upd, pre,
                  buf_a, buf_b, buf_c, fsrc, fbuf, req_src, req, nsrc, nbuf, rsrc, rbuf,
                  us, ss, gp, sig, pidx, lst, fpk,
                  sem_sa, sem_sb, sem_sc, sem_sf, sem_sn, sem_ra, sem_rb, sem_rc, sem_rf, sem_rn):
    g, i = lax.axis_index("grp"), lax.axis_index("blk")
    me = g * NBLK + i

    def mate(o):
        return (g, lax.rem(i + o, NBLK))

    def peer(o):
        return (lax.rem(g + o, NGRP), i)

    def far_dev(t):
        return lax.rem(g + 1 + t // NBLK, NGRP), lax.rem(i + t, NBLK)

    barrier = pltpu.get_barrier_semaphore()

    def greet(o, c):
        d = lax.rem(me + o, DEVICES)
        pl.semaphore_signal(barrier, inc=1, device_id=(d // NBLK, lax.rem(d, NBLK)), device_id_type=MESH)
        return c

    lax.fori_loop(1, DEVICES, greet, 0)

    owner_row = iota((DEVICES, NBR), 0)
    upper = bf(iota((NBR, NBR), 0) < iota((NBR, NBR), 1))
    before = jnp.zeros((DEVICES, 1), jnp.float32)
    wanted = jnp.zeros((DEVICES, LANES), jnp.float32)
    listed = jnp.zeros((8, NBR), jnp.float32)
    nt = (((1,), (1,)), ((), ()))
    for k in range(8):
        col = cols[8 + k : 9 + k, :]
        owner = lax.shift_right_logical(col, 8)
        row = col & 255
        hit = owner_row == owner
        one = jnp.where(hit, 1.0, 0.0)
        ahead = jnp.dot(one.astype(jnp.bfloat16), upper, preferred_element_type=jnp.float32) + before
        rank = jnp.sum(jnp.where(hit, ahead, 0.0), axis=0, keepdims=True).astype(jnp.int32)
        before = before + jnp.sum(one, axis=1, keepdims=True)
        place = owner * 16 + rank
        pidx[k : k + 1, :] = place
        rowf = row.astype(jnp.float32)
        ranked = jnp.where((owner_row & 15) == rank, rowf, 0.0).astype(jnp.bfloat16)
        wanted = wanted + lax.dot_general(one.astype(jnp.bfloat16), ranked, nt, preferred_element_type=jnp.float32)
        mine = bf(iota((NBR, NBR), 0) == place - g * NBR)
        rows8 = jnp.broadcast_to(rowf, (8, NBR)).astype(jnp.bfloat16)
        listed = listed + lax.dot_general(rows8, mine, nt, preferred_element_type=jnp.float32)
    req_src[...] = wanted.astype(jnp.int32)
    lst[...] = (lax.shift_right_logical(iota((8, NBR), 1), 4) * NBR + listed.astype(jnp.int32))[0:1]

    pl.semaphore_wait(barrier, DEVICES - 1)

    def ask(t, c):
        dg, di = far_dev(t)
        d = dg * NBLK + di
        pltpu.make_async_remote_copy(
            src_ref=req_src.at[pl.ds(d, 1)], dst_ref=req.at[pl.ds(me, 1)], send_sem=sem_sn.at[2], recv_sem=sem_rn.at[2],
            device_id=(dg, di), device_id_type=MESH).start()
        return c

    lax.fori_loop(0, 112, ask, 0)
    us[...] = jnp.zeros_like(us)
    us[0] = -res[...]
    rsrc[...] = jnp.zeros_like(rsrc)

    def whole(ref, rows, send, recv):
        return pltpu.make_async_remote_copy(
            src_ref=ref.at[pl.ds(0, rows)], dst_ref=ref.at[pl.ds(0, rows)], send_sem=send, recv_sem=recv,
            device_id=mate(1), device_id_type=MESH)

    asked = whole(req, 112, sem_sn.at[2], sem_rn.at[2])
    asked.wait_recv()
    asked.wait_send()

    order = (10, 9, 11, 6, 14, 5, 7, 13, 15, 2, 8, 1, 3, 4, 12)

    def spread(buf, send, recv):
        for o in order:
            y, z = i // 4, lax.rem(i, 4)
            to = lax.rem(y + o // 4, 4) * 4 + lax.rem(z + o % 4, 4)
            pltpu.make_async_remote_copy(
                src_ref=buf.at[i], dst_ref=buf.at[i], send_sem=send, recv_sem=recv,
                device_id=(g, to), device_id_type=MESH).start()

    def near_pick(buf):
        picked = []
        for q in range(16):
            if q < 14:
                idx = cols[1 + q // 2 : 2 + q // 2, q % 2 * LANES : (q % 2 + 1) * LANES] - g * (NBLK * NBR)
            else:
                idx = lst[:, (q - 14) * LANES : (q - 13) * LANES]
            idx = jnp.broadcast_to(idx, (8, LANES))
            lo, hi = idx & 127, lax.shift_right_logical(idx, 7)
            acc = jnp.zeros((8, LANES), jnp.float32)
            for v in range(32):
                acc = jnp.where(hi == v, lane_pick(buf[v // 2, :, v % 2 * LANES : (v % 2 + 1) * LANES], lo), acc)
            picked.append(acc)
        return picked

    def far_place(q):
        idx = jnp.broadcast_to(pidx[q // 2 : q // 2 + 1, q % 2 * LANES : (q % 2 + 1) * LANES], (8, LANES))
        return idx & 127, lax.shift_right_logical(idx, 7)

    def add_slot(acc, k, picked):
        return [x + jac[k, a] * picked for a, x in enumerate(acc)]

    def joined(first, second):
        return jnp.concatenate([first, second], axis=1)

    def near_couple(buf):
        picked = near_pick(buf)
        acc = [jnp.zeros((8, NBR), jnp.float32)] * 8
        for k in range(7):
            acc = add_slot(acc, 1 + k, joined(picked[2 * k], picked[2 * k + 1]))
        for k in range(8):
            got = []
            for h in range(2):
                lo, hi = far_place(2 * k + h)
                x = jnp.zeros((8, LANES), jnp.float32)
                for v in range(2):
                    x = jnp.where(hi == 2 * g + v, lane_pick(picked[14 + v], lo), x)
                got.append(x)
            acc = add_slot(acc, 8 + k, joined(*got))
        return fold_rows(acc)

    lane16 = iota((8, LANES), 1) & 15
    lane_group = lax.shift_right_logical(iota((8, LANES), 1), 4)
    turn = iota((8, LANES), 0) * 16 + lane16

    def step(j, carry):
        slot = lax.rem(j, 2)
        u = us[j]
        z = block_mul(dinv, u)
        buf_a[i, :, 0:NBR] = z
        sq = u * u
        buf_a[i, :, NBR : NBR + LANES] = sq[:, :LANES] + sq[:, LANES:]
        spread(buf_a, sem_sa, sem_ra)
        dots = []
        for l in range(6):
            t = u * us[l]
            dots.append(t[:, :LANES] + t[:, LANES:])
        zero = jnp.zeros((8, LANES), jnp.float32)
        gp[j] = fold_rows(dots + [zero, zero])
        done_a = whole(buf_a, 15, sem_sa, sem_ra)
        done_a.wait_recv()
        nsum = buf_a[0, :, NBR : NBR + LANES]
        for s in range(1, NBLK):
            nsum = nsum + buf_a[s, :, NBR : NBR + LANES]
        nrow = jnp.sum(nsum, axis=0, keepdims=True)
        nsrc[...] = nrow
        for o in range(1, NGRP):
            pltpu.make_async_remote_copy(
                src_ref=nsrc, dst_ref=nbuf.at[slot, g], send_sem=sem_sn.at[slot], recv_sem=sem_rn.at[slot],
                device_id=peer(o), device_id_type=MESH).start()
        nbuf[slot, g] = nrow
        coupled = near_couple(buf_a)
        z = block_mul(dinv, u - coupled)
        done_a.wait_send()
        buf_b[i] = z
        spread(buf_b, sem_sb, sem_rb)
        done_b = whole(buf_b, 15, sem_sb, sem_rb)
        done_b.wait_recv()
        coupled = near_couple(buf_b)
        z = block_mul(dinv, u - coupled)
        done_b.wait_send()
        buf_c[i] = z
        def far_send(t, c):
            dg = lax.rem(g + 1 + t // 2, NGRP)
            first = pl.multiple_of(dg * NBLK + lax.rem(t, 2) * 8, 8)
            idx = req[pl.ds(first, 8), :]
            lo, hi = idx & 127, lax.shift_right_logical(idx, 7)
            out = jnp.zeros((8, LANES), jnp.float32)
            for b in range(8):
                for h in range(2):
                    table = jnp.broadcast_to(buf_c[i, b : b + 1, h * LANES : (h + 1) * LANES], (8, LANES))
                    out = jnp.where((hi == h) & (lane_group == b), lane_pick(table, lo), out)
            fsrc[pl.ds(first, 8), :] = out
            for d in range(8):
                pltpu.make_async_remote_copy(
                    src_ref=fsrc.at[pl.ds(first + d, 1)], dst_ref=fbuf.at[slot, pl.ds(me, 1)],
                    send_sem=sem_sf, recv_sem=sem_rf.at[slot],
                    device_id=(dg, lax.rem(t, 2) * 8 + d), device_id_type=MESH).start()
            return c

        spread(buf_c, sem_sc, sem_rc)
        lax.fori_loop(0, 14, far_send, 0)
        ss[j] = z
        base = [jac[0, a] * z for a in range(8)]
        done_c = whole(buf_c, 15, sem_sc, sem_rc)
        done_c.wait_recv()
        picked = near_pick(buf_c)
        acc = base
        for k in range(7):
            acc = add_slot(acc, 1 + k, joined(picked[2 * k], picked[2 * k + 1]))
        done_c.wait_send()
        done_f = pltpu.make_async_remote_copy(
            src_ref=fsrc.at[pl.ds(0, 112)], dst_ref=fbuf.at[slot, pl.ds(0, 112)], send_sem=sem_sf, recv_sem=sem_rf.at[slot],
            device_id=mate(1), device_id_type=MESH)
        done_f.wait_recv()
        for q in range(16):
            x = jnp.zeros((8, LANES), jnp.float32)
            for o in range(8):
                rowv = jnp.broadcast_to(fbuf[slot, 8 * q + o : 8 * q + o + 1, :], (8, LANES))
                x = jnp.where(lane_group == o, lane_pick(rowv, turn), x)
            fpk[q] = x
        fpk[2 * g] = picked[14]
        fpk[2 * g + 1] = picked[15]
        for k in range(8):
            got = []
            for h in range(2):
                lo, hi = far_place(2 * k + h)
                x = jnp.zeros((8, LANES), jnp.float32)
                for v in range(16):
                    x = jnp.where(hi == v, lane_pick(fpk[v], lo), x)
                got.append(x)
            acc = add_slot(acc, 8 + k, joined(*got))
        image = fold_rows(acc)
        done_f.wait_send()
        done_n = pltpu.make_async_remote_copy(
            src_ref=nbuf.at[slot, pl.ds(0, 7)], dst_ref=nbuf.at[slot, pl.ds(0, 7)], send_sem=sem_sn.at[slot], recv_sem=sem_rn.at[slot],
            device_id=mate(1), device_id_type=MESH)
        done_n.wait_recv()
        done_n.wait_send()
        total = nbuf[slot, 0]
        for s in range(1, NGRP):
            total = total + nbuf[slot, s]
        scale = lax.rsqrt(jnp.maximum(jnp.sum(total, axis=1, keepdims=True), 1e-12))
        sig[j] = jnp.broadcast_to(scale, (8, LANES))
        us[j + 1] = (image - u) * scale
        return carry

    lax.fori_loop(0, KRYLOV, step, 0)

    u = us[KRYLOV]
    dots = []
    for l in range(6):
        t = u * us[l]
        dots.append(t[:, :LANES] + t[:, LANES:])
    zero = jnp.zeros((8, LANES), jnp.float32)
    gp[KRYLOV] = fold_rows(dots + [zero, zero])
    row = jnp.zeros((1, LANES), jnp.float32)
    lane = iota((8, LANES), 1)
    sub = iota((8, LANES), 0)
    for j in range(6):
        s = jnp.sum(gp[j], axis=1, keepdims=True)
        row = row + jnp.sum(jnp.where(lane == 8 * j + sub, s, 0.0), axis=0, keepdims=True)
    rsrc[...] = row

    def tell(o, c):
        d = lax.rem(me + o, DEVICES)
        pltpu.make_async_remote_copy(
            src_ref=rsrc, dst_ref=rbuf.at[pl.ds(me, 1)], send_sem=sem_sf, recv_sem=sem_rf.at[2],
            device_id=(d // NBLK, lax.rem(d, NBLK)), device_id_type=MESH).start()
        return c

    lax.fori_loop(1, DEVICES, tell, 0)
    rbuf[pl.ds(me, 1), :] = row
    done = whole(rbuf, 127, sem_sf, sem_rf.at[2])
    done.wait_recv()
    done.wait_send()
    total = rbuf[0:8, :]
    for q in range(1, 16):
        total = total + rbuf[8 * q : 8 * q + 8, :]
    total = jnp.sum(total, axis=0, keepdims=True)
    gram = [[jnp.broadcast_to(total[:, 8 * j + l : 8 * j + l + 1], (8, LANES)) for l in range(j + 1)] for j in range(6)]
    weights = small_solve(gram, [sig[j] for j in range(KRYLOV)])
    for h in range(2):
        part = slice(h * LANES, (h + 1) * LANES)
        x = weights[0] * ss[0, :, part]
        for l in range(1, KRYLOV):
            x = x + weights[l] * ss[l, :, part]
        upd[:, part] = x
    pre[...] = ss[0]


def krylov(jacobian, inverse, newton_residual, block_cols):
    vm = pl.BlockSpec(memory_space=pltpu.VMEM)
    f32, i32 = jnp.float32, jnp.int32
    dma = pltpu.SemaphoreType.DMA
    return pl.pallas_call(
        krylov_kernel,
        out_shape=(jax.ShapeDtypeStruct((8, NBR), f32), jax.ShapeDtypeStruct((8, NBR), f32)),
        in_specs=[vm] * 4,
        out_specs=(vm, vm),
        scratch_shapes=[
            pltpu.VMEM((NBLK, 8, NBR + LANES), f32),
            pltpu.VMEM((NBLK, 8, NBR), f32),
            pltpu.VMEM((NBLK, 8, NBR), f32),
            pltpu.VMEM((DEVICES, LANES), f32),
            pltpu.VMEM((2, DEVICES, LANES), f32),
            pltpu.VMEM((DEVICES, LANES), i32),
            pltpu.VMEM((DEVICES, LANES), i32),
            pltpu.VMEM((1, LANES), f32),
            pltpu.VMEM((2, NGRP, 1, LANES), f32),
            pltpu.VMEM((1, LANES), f32),
            pltpu.VMEM((DEVICES, LANES), f32),
            pltpu.VMEM((KRYLOV + 1, 8, NBR), f32),
            pltpu.VMEM((KRYLOV, 8, NBR), f32),
            pltpu.VMEM((KRYLOV + 1, 8, LANES), f32),
            pltpu.VMEM((KRYLOV, 8, LANES), f32),
            pltpu.VMEM((8, NBR), i32),
            pltpu.VMEM((1, NBR), i32),
            pltpu.VMEM((16, 8, LANES), f32),
            dma, dma, dma, dma, dma((3,)), dma, dma, dma, dma((3,)), dma((3,)),
        ],
        compiler_params=pltpu.CompilerParams(collective_id=0, has_side_effects=True, vmem_limit_bytes=32 * 1024 * 1024),
    )(jacobian, inverse, newton_residual, block_cols)


GRP = ("grp",)
BLK = ("blk",)
GRP_BLK = ("grp", "blk")


def sent_together(arrays, axis, split_dim, concat_dim, along):
    columns = [a.reshape(*a.shape[:along], -1) for a in arrays]
    both = jnp.concatenate(columns, axis=along)
    result, at, done = (
        lax.all_to_all(both, axis, split_axis=split_dim, concat_axis=concat_dim, tiled=True),
        0,
        [],
    )
    for a, column in zip(arrays, columns):
        piece = result[..., at : at + column.shape[along]]
        done.append(piece.reshape(*piece.shape[:along], *a.shape[along:]))
        at += column.shape[along]
    return tuple(done)


def passed_along(block, axis, distance):
    devices = range(lax.axis_size(axis))
    route = [((i - distance) % len(devices), i) for i in devices]
    return lax.ppermute(block, axis, route)


def invert_blocks(diag):
    size = diag.shape[0]
    eye_mat = jnp.eye(size, dtype=jnp.float32)[:, :, None]
    inverse = eye_mat * jnp.ones_like(diag[:1])
    work = diag
    for pivot_row in range(size):
        scale = 1.0 / work[pivot_row, pivot_row]
        top_work = work[pivot_row] * scale
        top_inverse = inverse[pivot_row] * scale
        factor = work[:, pivot_row]
        work = work - factor[:, None, :] * top_work[None]
        inverse = inverse - factor[:, None, :] * top_inverse[None]
        work = work.at[pivot_row].set(top_work)
        inverse = inverse.at[pivot_row].set(top_inverse)
    return inverse


def add_stamps(summed, values, targets, counts, offset, local_rows):
    slots = values.shape[2]
    slot_ids = offset + jnp.arange(slots, dtype=jnp.int32)
    live = slot_ids[None, :] < counts
    masked = jnp.where(live[:, None, :], values, 0.0)
    index_pairs = jnp.stack([targets // local_rows, targets % local_rows], axis=2).astype(jnp.int32)
    numbers = lax.ScatterDimensionNumbers(
        update_window_dims=(1,), inserted_window_dims=(0, 2), scatter_dims_to_operand_dims=(0, 2)
    )
    return lax.scatter_add(summed, index_pairs, masked, numbers)


def local(stamps, stamp_target, pair_counts, conductance, block_cols, newton_residual):
    grp_count = lax.axis_size(GRP)
    blk_count = lax.axis_size(BLK)
    devices = grp_count * blk_count
    local_rows = conductance.shape[1]
    capacity = stamps.shape[3]
    summed = jnp.zeros((K, 64, local_rows), jnp.float32)
    front = capacity // 4
    got_values, got_target, got_counts = (
        lax.all_to_all(stamps[:, :, :, :front], GRP_BLK, split_axis=1, concat_axis=0, tiled=True),
        *sent_together((stamp_target[:, :, :front], pair_counts), GRP_BLK, 1, 0, 2),
    )
    summed = add_stamps(
        summed,
        got_values.reshape(devices, 64, front),
        got_target.reshape(devices, front),
        got_counts,
        0,
        local_rows,
    )
    my_index = lax.axis_index(GRP_BLK)
    next_index = (my_index + 1) % devices
    own_values = lax.dynamic_index_in_dim(stamps[0], my_index, 0, keepdims=False)[:, front:]
    own_target = lax.dynamic_index_in_dim(stamp_target[0], my_index, 0, keepdims=False)[front:]
    own_count = lax.dynamic_index_in_dim(pair_counts[0], my_index, 0, keepdims=True)
    next_values = lax.dynamic_index_in_dim(stamps[0], next_index, 0, keepdims=False)[:, front:]
    next_target = lax.dynamic_index_in_dim(stamp_target[0], next_index, 0, keepdims=False)[front:]
    next_count = lax.dynamic_index_in_dim(pair_counts[0], next_index, 0, keepdims=True)
    prior_values, prior_target, prior_count = passed_along(
        (next_values, next_target, next_count), GRP_BLK, 1
    )
    tail_values = jnp.stack([own_values, prior_values], axis=0)
    tail_target = jnp.stack([own_target, prior_target], axis=0)
    tail_counts = jnp.stack([own_count, prior_count], axis=0)
    summed = add_stamps(summed, tail_values, tail_target, tail_counts, front, local_rows)
    jacobian = summed.reshape(K, 8, 8, local_rows)
    identity = jnp.eye(8, dtype=jnp.float32)
    jacobian = jacobian.at[0].add(identity[:, :, None] * conductance[:, None, :])
    inverse = invert_blocks(jacobian[0])
    update, preconditioned = krylov(jacobian, inverse, newton_residual, block_cols)
    return update, jacobian, preconditioned


def solution(mesh):
    return jax.shard_map(
        local,
        mesh=mesh,
        in_specs=(
            P(GRP_BLK, None, None, None),
            P(GRP_BLK, None, None),
            P(GRP_BLK, None),
            P(None, GRP_BLK),
            P(None, GRP_BLK),
            P(None, GRP_BLK),
        ),
        out_specs=(P(None, GRP_BLK), P(None, None, None, GRP_BLK), P(None, GRP_BLK)),
        check_vma=False,
    )
```

```python
import functools
import jax
import jax.numpy as jnp
from jax import lax
from jax.experimental import pallas as pl
from jax.experimental.pallas import tpu as pltpu
from jax.sharding import PartitionSpec as P

K = 16
KRYLOV = 5
NBR = 256
NGRP = 8
NBLK = 16
DEVICES = 128
LANES = 128
FRONT = 32
EPS = 1e-06
MESH = pl.DeviceIdType.MESH
AXES = ("grp", "blk")


def bf(x):
    return x.astype(jnp.float32).astype(jnp.bfloat16)


def iota(shape, dim):
    return lax.broadcasted_iota(jnp.int32, shape, dim)


def lane_pick(table, index):
    return jnp.take_along_axis(table, index, axis=1, mode="promise_in_bounds")


def fold_rows(parts):
    row = iota(parts[0].shape, 0)
    step = 1
    while len(parts) > 1:
        even = (row & step) == 0
        merged = []
        for first, second in zip(parts[0::2], parts[1::2]):
            kept = jnp.where(even, first, second)
            moved = jnp.where(even, second, first)
            merged.append(kept + pltpu.roll(moved, step, 0))
        parts = merged
        step *= 2
    return parts[0]


def block_mul(blocks, vector):
    return fold_rows([blocks[a] * vector for a in range(8)])


def small_solve(gram, scales):
    inv = [1.0 / s for s in scales] + [1.0]
    sc = list(scales) + [1.0]
    n = KRYLOV + 1
    g = [[None] * n for _ in range(n)]
    for l in range(n):
        for m in range(l + 1):
            val = gram[l][m] * sc[l] * sc[m]
            g[l][m] = val
            g[m][l] = val
    beta = jnp.sqrt(gram[0][0] + EPS)
    basis = [[inv[0] / beta]]
    hess = []
    for j in range(KRYLOV):
        b = basis[j]
        w = [None] * (j + 2)
        for l in range(j + 1):
            w[l] = b[l] if w[l] is None else w[l] + b[l]
            w[l + 1] = b[l] * inv[l + 1]
        gw = []
        for l in range(j + 2):
            t = g[l][0] * w[0]
            for m in range(1, j + 2):
                t = t + g[l][m] * w[m]
            gw.append(t)
        column = []
        for i in range(j + 1):
            t = basis[i][0] * gw[0]
            for l in range(1, i + 1):
                t = t + basis[i][l] * gw[l]
            column.append(t)
        for i in range(j + 1):
            for l in range(i + 1):
                w[l] = w[l] - column[i] * basis[i][l]
        sq = None
        for l in range(j + 2):
            t = g[l][0] * w[0]
            for m in range(1, j + 2):
                t = t + g[l][m] * w[m]
            sq = t * w[l] if sq is None else sq + t * w[l]
        length = jnp.sqrt(jnp.maximum(sq, 0.0) + EPS)
        column.append(length)
        hess.append(column)
        scale = 1.0 / length
        basis.append([x * scale for x in w])
    work = [[None] * KRYLOV for _ in range(KRYLOV)]
    for p in range(KRYLOV):
        for q in range(p + 1):
            t = hess[p][0] * hess[q][0]
            for i in range(1, q + 2):
                t = t + hess[p][i] * hess[q][i]
            work[p][q] = t
            work[q][p] = t
    vec = [beta * hess[p][0] for p in range(KRYLOV)]
    for p in range(KRYLOV):
        scale = 1.0 / work[p][p]
        top = [x * scale for x in work[p]]
        tv = vec[p] * scale
        for q in range(KRYLOV):
            if q == p:
                continue
            f = work[q][p]
            work[q] = [x - f * y for x, y in zip(work[q], top)]
            vec[q] = vec[q] - f * tv
        work[p] = top
        vec[p] = tv
    out = []
    for l in range(KRYLOV):
        t = None
        for j in range(l, KRYLOV):
            x = vec[j] * basis[j][l]
            t = x if t is None else t + x
        out.append(t * sc[l])
    return out


def solver_kernel(stamps, target, counts, cond, res, cols, upd, jac_out, pre,
                  stage, sbuf, rbuf_s, trep, cntb, tail, ttail, ttsrc, jac, dinv, sem_h, sem_ss, sem_rs, sem_t, sem_j,
                  buf_a, buf_b, buf_c, fsrc, fbuf, req_src, req, nsrc, nbuf, rsrc, rbuf,
                  us, ss, gp, sig, pidx, lst, fpk,
                  sem_sa, sem_sb, sem_sc, sem_sf, sem_sn, sem_ra, sem_rb, sem_rc, sem_rf, sem_rn):
    g, i = lax.axis_index("grp"), lax.axis_index("blk")
    me = g * NBLK + i

    def mate(o):
        return (g, lax.rem(i + o, NBLK))

    def peer(o):
        return (lax.rem(g + o, NGRP), i)

    def far_dev(t):
        return lax.rem(g + 1 + t // NBLK, NGRP), lax.rem(i + t, NBLK)

    barrier = pltpu.get_barrier_semaphore()

    def greet(o, c):
        d = lax.rem(me + o, DEVICES)
        pl.semaphore_signal(barrier, inc=1, device_id=(d // NBLK, lax.rem(d, NBLK)), device_id_type=MESH)
        return c

    lax.fori_loop(1, DEVICES, greet, 0)

    my_chunk = me // 8

    def load(t):
        first = pl.multiple_of(lax.rem(my_chunk + t, 16) * 8, 8)
        return pltpu.make_async_copy(stamps.at[0, pl.ds(first, 8)], stage.at[pl.ds(first, 8)], sem_h.at[t])

    def start_load(t, c):
        load(t).start()
        return c

    lax.fori_loop(0, 16, start_load, 0)
    lane_big = iota((DEVICES, LANES), 1)
    row_big = iota((DEVICES, LANES), 0)
    count = jnp.sum(jnp.where(lane_big == row_big, counts[...], 0), axis=1, keepdims=True)
    count = jnp.broadcast_to(count, (DEVICES, LANES))
    cntb[...] = count
    tgt = jnp.where((lane_big < count) & (row_big != me), target[...], -1)
    trep[...] = lane_pick(tgt, lane_big & (FRONT - 1)).astype(jnp.float32)
    nxt = lax.rem(me + 1, DEVICES)
    lane1 = iota((1, LANES), 1)
    ttsrc[...] = jnp.where((lane1 >= FRONT) & (lane1 < cntb[pl.ds(nxt, 1), :]), target[pl.ds(nxt, 1), :], -1).astype(jnp.float32)
    own_target = jnp.where(lane1 < cntb[pl.ds(me, 1), :], target[pl.ds(me, 1), :], -1)
    quarter = lax.shift_right_logical(iota((16, LANES), 1), 5)

    def pack(first):
        rows = trep[pl.ds(first, 8), :]
        for e in range(8):
            x = stage[first + e, 0:16, :]
            for q in range(1, 4):
                x = jnp.where(quarter == q, pltpu.roll(stage[first + e, 16 * q : 16 * q + 16, :], 32 * q, 1), x)
            sbuf[first + e, 0:16, :] = x
            sbuf[first + e, 16:17, :] = rows[e : e + 1]

    def stamp_copy(d):
        return pltpu.make_async_remote_copy(
            src_ref=sbuf.at[d, pl.ds(0, 17)], dst_ref=rbuf_s.at[me, pl.ds(0, 17)], send_sem=sem_ss, recv_sem=sem_rs.at[my_chunk],
            device_id=(d // NBLK, lax.rem(d, NBLK)), device_id_type=MESH)

    load(0).wait()
    own_first = pl.multiple_of(my_chunk * 8, 8)
    pack(own_first)
    rbuf_s[me] = sbuf[me]
    pl.semaphore_wait(barrier, DEVICES - 1)
    for e in range(1, 8):
        stamp_copy(own_first + lax.rem(me + e, 8)).start()

    def send_chunk(t, c):
        load(t).wait()
        first = pl.multiple_of(lax.rem(my_chunk + t, 16) * 8, 8)
        pack(first)
        for e in range(8):
            stamp_copy(first + lax.rem(me + e, 8)).start()
        return c

    lax.fori_loop(1, 16, send_chunk, 0)
    tail_dev = (nxt // NBLK, lax.rem(nxt, NBLK))
    tail_copy = pltpu.make_async_remote_copy(
        src_ref=stage.at[nxt], dst_ref=tail, send_sem=sem_t.at[0], recv_sem=sem_t.at[1], device_id=tail_dev, device_id_type=MESH)
    tail_copy.start()
    ttail_copy = pltpu.make_async_remote_copy(
        src_ref=ttsrc, dst_ref=ttail, send_sem=sem_t.at[2], recv_sem=sem_t.at[3], device_id=tail_dev, device_id_type=MESH)
    ttail_copy.start()

    owner_row = iota((DEVICES, NBR), 0)
    upper = bf(iota((NBR, NBR), 0) < iota((NBR, NBR), 1))
    before = jnp.zeros((DEVICES, 1), jnp.float32)
    wanted = jnp.zeros((DEVICES, LANES), jnp.float32)
    listed = jnp.zeros((8, NBR), jnp.float32)
    nt = (((1,), (1,)), ((), ()))
    for k in range(8):
        col = cols[8 + k : 9 + k, :]
        owner = lax.shift_right_logical(col, 8)
        row = col & 255
        hit = owner_row == owner
        one = jnp.where(hit, 1.0, 0.0)
        ahead = jnp.dot(one.astype(jnp.bfloat16), upper, preferred_element_type=jnp.float32) + before
        rank = jnp.sum(jnp.where(hit, ahead, 0.0), axis=0, keepdims=True).astype(jnp.int32)
        before = before + jnp.sum(one, axis=1, keepdims=True)
        place = owner * 16 + rank
        pidx[k : k + 1, :] = place
        rowf = row.astype(jnp.float32)
        ranked = jnp.where((owner_row & 15) == rank, rowf, 0.0).astype(jnp.bfloat16)
        wanted = wanted + lax.dot_general(one.astype(jnp.bfloat16), ranked, nt, preferred_element_type=jnp.float32)
        mine = bf(iota((NBR, NBR), 0) == place - g * NBR)
        rows8 = jnp.broadcast_to(rowf, (8, NBR)).astype(jnp.bfloat16)
        listed = listed + lax.dot_general(rows8, mine, nt, preferred_element_type=jnp.float32)
    req_src[...] = wanted.astype(jnp.int32)
    lst[...] = (lax.shift_right_logical(iota((8, NBR), 1), 4) * NBR + listed.astype(jnp.int32))[0:1]

    def ask(t, c):
        dg, di = far_dev(t)
        d = dg * NBLK + di
        pltpu.make_async_remote_copy(
            src_ref=req_src.at[pl.ds(d, 1)], dst_ref=req.at[pl.ds(me, 1)], send_sem=sem_sn.at[2], recv_sem=sem_rn.at[2],
            device_id=(dg, di), device_id_type=MESH).start()
        return c

    lax.fori_loop(0, 112, ask, 0)
    us[...] = jnp.zeros_like(us)
    us[0] = -res[...]
    rsrc[...] = jnp.zeros_like(rsrc)

    def whole(ref, rows, send, recv):
        return pltpu.make_async_remote_copy(
            src_ref=ref.at[pl.ds(0, rows)], dst_ref=ref.at[pl.ds(0, rows)], send_sem=send, recv_sem=recv,
            device_id=mate(1), device_id_type=MESH)

    jac[...] = jnp.zeros_like(jac)
    node = iota((NBR, NBR), 0)

    def add_slots(values, goal):
        slot_k = lax.shift_right_arithmetic(goal, 8)
        values = jnp.where(goal >= 0, values, 0.0)
        high = values.astype(jnp.bfloat16)
        low = (values - high.astype(jnp.float32)).astype(jnp.bfloat16)
        both = jnp.concatenate([high, low], axis=1)
        there = bf(node == (goal & 255))
        there = jnp.concatenate([there, there], axis=1)
        twice = jnp.concatenate([slot_k, slot_k], axis=1)
        for k0 in range(0, K, 4):
            rows = [both * bf(jnp.broadcast_to(twice == k0 + k, (64, 2 * NBR))) for k in range(4)]
            part = lax.dot_general(jnp.concatenate(rows, axis=0), there, nt, preferred_element_type=jnp.float32)
            jac[k0 : k0 + 4] = jac[k0 : k0 + 4] + part.reshape(4, 8, 8, NBR)

    def add_chunk(first):
        wide, goals = [], []
        for tile in range(2):
            blocks = [rbuf_s[first + 4 * tile + s, 0:16, :] for s in range(4)]
            parts = []
            for q in range(4):
                x = None
                for s in range(4):
                    y = blocks[s] if s == q else pltpu.roll(blocks[s], (s - q) * 32 % LANES, 1)
                    x = y if x is None else jnp.where(quarter == s, y, x)
                parts.append(x)
            wide.append(jnp.concatenate(parts, axis=0))
            x = rbuf_s[first + 4 * tile, 16:17, :]
            for s in range(1, 4):
                x = jnp.where(quarter[0:1] == s, rbuf_s[first + 4 * tile + s, 16:17, :], x)
            goals.append(x.astype(jnp.int32))
        add_slots(jnp.concatenate(wide, axis=1), jnp.concatenate(goals, axis=1))

    def chunk_wait(first, count, sem):
        return pltpu.make_async_remote_copy(
            src_ref=sbuf.at[pl.ds(0, count), pl.ds(0, 17)], dst_ref=rbuf_s.at[pl.ds(0, count), pl.ds(0, 17)],
            send_sem=sem_ss, recv_sem=sem, device_id=mate(1), device_id_type=MESH)

    chunk_wait(own_first, 7, sem_rs.at[my_chunk]).wait_recv()
    add_chunk(own_first)

    def take_chunk(t, c):
        chunk = lax.rem(my_chunk + 16 - t, 16)
        first = pl.multiple_of(chunk * 8, 8)
        chunk_wait(first, 8, sem_rs.at[chunk]).wait_recv()
        add_chunk(first)
        return c

    lax.fori_loop(1, 16, take_chunk, 0)
    tail_copy.wait_recv()
    ttail_copy.wait_recv()
    add_slots(
        jnp.concatenate([stage[me], tail[...]], axis=1),
        jnp.concatenate([own_target, ttail[...].astype(jnp.int32)], axis=1))
    sub8 = iota((8, NBR), 0)
    for a in range(8):
        jac[0, a] = jac[0, a] + jnp.where(sub8 == a, jnp.broadcast_to(cond[a : a + 1, :], (8, NBR)), 0.0)
    jac_copy = pltpu.make_async_copy(jac, jac_out, sem_j)
    jac_copy.start()

    work = [jac[0, a] for a in range(8)]
    inverse = [jnp.where(sub8 == a, 1.0, 0.0) for a in range(8)]
    for p in range(8):
        scale = 1.0 / work[p][p : p + 1, :]
        top_w, top_i = work[p] * scale, inverse[p] * scale
        for a in range(8):
            if a != p:
                factor = work[a][p : p + 1, :]
                work[a] = work[a] - factor * top_w
                inverse[a] = inverse[a] - factor * top_i
        work[p], inverse[p] = top_w, top_i
    for a in range(8):
        dinv[a] = inverse[a]
    chunk_wait(own_first, 127, sem_ss).wait_send()
    tail_copy.wait_send()
    ttail_copy.wait_send()
    asked = whole(req, 112, sem_sn.at[2], sem_rn.at[2])
    asked.wait_recv()
    asked.wait_send()

    order = (10, 9, 11, 6, 14, 5, 7, 13, 15, 2, 8, 1, 3, 4, 12)

    def spread(buf, send, recv):
        for o in order:
            y, z = i // 4, lax.rem(i, 4)
            to = lax.rem(y + o // 4, 4) * 4 + lax.rem(z + o % 4, 4)
            pltpu.make_async_remote_copy(
                src_ref=buf.at[i], dst_ref=buf.at[i], send_sem=send, recv_sem=recv,
                device_id=(g, to), device_id_type=MESH).start()

    def near_pick(buf):
        picked = []
        for q in range(16):
            if q < 14:
                idx = cols[1 + q // 2 : 2 + q // 2, q % 2 * LANES : (q % 2 + 1) * LANES] - g * (NBLK * NBR)
            else:
                idx = lst[:, (q - 14) * LANES : (q - 13) * LANES]
            idx = jnp.broadcast_to(idx, (8, LANES))
            lo, hi = idx & 127, lax.shift_right_logical(idx, 7)
            acc = jnp.zeros((8, LANES), jnp.float32)
            for v in range(32):
                acc = jnp.where(hi == v, lane_pick(buf[v // 2, :, v % 2 * LANES : (v % 2 + 1) * LANES], lo), acc)
            picked.append(acc)
        return picked

    def far_place(q):
        idx = jnp.broadcast_to(pidx[q // 2 : q // 2 + 1, q % 2 * LANES : (q % 2 + 1) * LANES], (8, LANES))
        return idx & 127, lax.shift_right_logical(idx, 7)

    def add_slot(acc, k, picked):
        return [x + jac[k, a] * picked for a, x in enumerate(acc)]

    def joined(first, second):
        return jnp.concatenate([first, second], axis=1)

    def near_couple(buf):
        picked = near_pick(buf)
        acc = [jnp.zeros((8, NBR), jnp.float32)] * 8
        for k in range(7):
            acc = add_slot(acc, 1 + k, joined(picked[2 * k], picked[2 * k + 1]))
        for k in range(8):
            got = []
            for h in range(2):
                lo, hi = far_place(2 * k + h)
                x = jnp.zeros((8, LANES), jnp.float32)
                for v in range(2):
                    x = jnp.where(hi == 2 * g + v, lane_pick(picked[14 + v], lo), x)
                got.append(x)
            acc = add_slot(acc, 8 + k, joined(*got))
        return fold_rows(acc)

    lane16 = iota((8, LANES), 1) & 15
    lane_group = lax.shift_right_logical(iota((8, LANES), 1), 4)
    turn = iota((8, LANES), 0) * 16 + lane16

    def step(j, carry):
        slot = lax.rem(j, 2)
        u = us[j]
        z = block_mul(dinv, u)
        buf_a[i, :, 0:NBR] = z
        sq = u * u
        buf_a[i, :, NBR : NBR + LANES] = sq[:, :LANES] + sq[:, LANES:]
        spread(buf_a, sem_sa, sem_ra)
        dots = []
        for l in range(6):
            t = u * us[l]
            dots.append(t[:, :LANES] + t[:, LANES:])
        zero = jnp.zeros((8, LANES), jnp.float32)
        gp[j] = fold_rows(dots + [zero, zero])
        done_a = whole(buf_a, 15, sem_sa, sem_ra)
        done_a.wait_recv()
        nsum = buf_a[0, :, NBR : NBR + LANES]
        for s in range(1, NBLK):
            nsum = nsum + buf_a[s, :, NBR : NBR + LANES]
        nrow = jnp.sum(nsum, axis=0, keepdims=True)
        nsrc[...] = nrow
        for o in range(1, NGRP):
            pltpu.make_async_remote_copy(
                src_ref=nsrc, dst_ref=nbuf.at[slot, g], send_sem=sem_sn.at[slot], recv_sem=sem_rn.at[slot],
                device_id=peer(o), device_id_type=MESH).start()
        nbuf[slot, g] = nrow
        coupled = near_couple(buf_a)
        z = block_mul(dinv, u - coupled)
        done_a.wait_send()
        buf_b[i] = z
        spread(buf_b, sem_sb, sem_rb)
        done_b = whole(buf_b, 15, sem_sb, sem_rb)
        done_b.wait_recv()
        coupled = near_couple(buf_b)
        z = block_mul(dinv, u - coupled)
        done_b.wait_send()
        buf_c[i] = z
        def far_send(t, c):
            dg = lax.rem(g + 1 + t // 2, NGRP)
            first = pl.multiple_of(dg * NBLK + lax.rem(t, 2) * 8, 8)
            idx = req[pl.ds(first, 8), :]
            lo, hi = idx & 127, lax.shift_right_logical(idx, 7)
            out = jnp.zeros((8, LANES), jnp.float32)
            for b in range(8):
                for h in range(2):
                    table = jnp.broadcast_to(buf_c[i, b : b + 1, h * LANES : (h + 1) * LANES], (8, LANES))
                    out = jnp.where((hi == h) & (lane_group == b), lane_pick(table, lo), out)
            fsrc[pl.ds(first, 8), :] = out
            for d in range(8):
                pltpu.make_async_remote_copy(
                    src_ref=fsrc.at[pl.ds(first + d, 1)], dst_ref=fbuf.at[slot, pl.ds(me, 1)],
                    send_sem=sem_sf, recv_sem=sem_rf.at[slot],
                    device_id=(dg, lax.rem(t, 2) * 8 + d), device_id_type=MESH).start()
            return c

        spread(buf_c, sem_sc, sem_rc)
        lax.fori_loop(0, 14, far_send, 0)
        ss[j] = z
        base = [jac[0, a] * z for a in range(8)]
        done_c = whole(buf_c, 15, sem_sc, sem_rc)
        done_c.wait_recv()
        picked = near_pick(buf_c)
        acc = base
        for k in range(7):
            acc = add_slot(acc, 1 + k, joined(picked[2 * k], picked[2 * k + 1]))
        done_c.wait_send()
        done_f = pltpu.make_async_remote_copy(
            src_ref=fsrc.at[pl.ds(0, 112)], dst_ref=fbuf.at[slot, pl.ds(0, 112)], send_sem=sem_sf, recv_sem=sem_rf.at[slot],
            device_id=mate(1), device_id_type=MESH)
        done_f.wait_recv()
        for q in range(16):
            x = jnp.zeros((8, LANES), jnp.float32)
            for o in range(8):
                rowv = jnp.broadcast_to(fbuf[slot, 8 * q + o : 8 * q + o + 1, :], (8, LANES))
                x = jnp.where(lane_group == o, lane_pick(rowv, turn), x)
            fpk[q] = x
        fpk[2 * g] = picked[14]
        fpk[2 * g + 1] = picked[15]
        for k in range(8):
            got = []
            for h in range(2):
                lo, hi = far_place(2 * k + h)
                x = jnp.zeros((8, LANES), jnp.float32)
                for v in range(16):
                    x = jnp.where(hi == v, lane_pick(fpk[v], lo), x)
                got.append(x)
            acc = add_slot(acc, 8 + k, joined(*got))
        image = fold_rows(acc)
        done_f.wait_send()
        done_n = pltpu.make_async_remote_copy(
            src_ref=nbuf.at[slot, pl.ds(0, 7)], dst_ref=nbuf.at[slot, pl.ds(0, 7)], send_sem=sem_sn.at[slot], recv_sem=sem_rn.at[slot],
            device_id=mate(1), device_id_type=MESH)
        done_n.wait_recv()
        done_n.wait_send()
        total = nbuf[slot, 0]
        for s in range(1, NGRP):
            total = total + nbuf[slot, s]
        scale = lax.rsqrt(jnp.maximum(jnp.sum(total, axis=1, keepdims=True), 1e-12))
        sig[j] = jnp.broadcast_to(scale, (8, LANES))
        us[j + 1] = (image - u) * scale
        return carry

    lax.fori_loop(0, KRYLOV, step, 0)

    u = us[KRYLOV]
    dots = []
    for l in range(6):
        t = u * us[l]
        dots.append(t[:, :LANES] + t[:, LANES:])
    zero = jnp.zeros((8, LANES), jnp.float32)
    gp[KRYLOV] = fold_rows(dots + [zero, zero])
    row = jnp.zeros((1, LANES), jnp.float32)
    lane = iota((8, LANES), 1)
    sub = iota((8, LANES), 0)
    for j in range(6):
        s = jnp.sum(gp[j], axis=1, keepdims=True)
        row = row + jnp.sum(jnp.where(lane == 8 * j + sub, s, 0.0), axis=0, keepdims=True)
    rsrc[...] = row

    def tell(o, c):
        d = lax.rem(me + o, DEVICES)
        pltpu.make_async_remote_copy(
            src_ref=rsrc, dst_ref=rbuf.at[pl.ds(me, 1)], send_sem=sem_sf, recv_sem=sem_rf.at[2],
            device_id=(d // NBLK, lax.rem(d, NBLK)), device_id_type=MESH).start()
        return c

    lax.fori_loop(1, DEVICES, tell, 0)
    rbuf[pl.ds(me, 1), :] = row
    done = whole(rbuf, 127, sem_sf, sem_rf.at[2])
    done.wait_recv()
    done.wait_send()
    total = rbuf[0:8, :]
    for q in range(1, 16):
        total = total + rbuf[8 * q : 8 * q + 8, :]
    total = jnp.sum(total, axis=0, keepdims=True)
    gram = [[jnp.broadcast_to(total[:, 8 * j + l : 8 * j + l + 1], (8, LANES)) for l in range(j + 1)] for j in range(6)]
    weights = small_solve(gram, [sig[j] for j in range(KRYLOV)])
    for h in range(2):
        part = slice(h * LANES, (h + 1) * LANES)
        x = weights[0] * ss[0, :, part]
        for l in range(1, KRYLOV):
            x = x + weights[l] * ss[l, :, part]
        upd[:, part] = x
    pre[...] = ss[0]
    jac_copy.wait()


def local(stamps, stamp_target, pair_counts, conductance, block_cols, newton_residual):
    vm = pl.BlockSpec(memory_space=pltpu.VMEM)
    hbm = pl.BlockSpec(memory_space=pl.ANY)
    f32, i32 = jnp.float32, jnp.int32
    dma = pltpu.SemaphoreType.DMA
    return pl.pallas_call(
        solver_kernel,
        out_shape=(
            jax.ShapeDtypeStruct((8, NBR), f32),
            jax.ShapeDtypeStruct((K, 8, 8, NBR), f32),
            jax.ShapeDtypeStruct((8, NBR), f32),
        ),
        in_specs=[hbm] + [vm] * 5,
        out_specs=(vm, hbm, vm),
        scratch_shapes=[
            pltpu.VMEM((DEVICES, 64, LANES), f32),
            pltpu.VMEM((DEVICES, 24, LANES), f32),
            pltpu.VMEM((DEVICES, 24, LANES), f32),
            pltpu.VMEM((DEVICES, LANES), f32),
            pltpu.VMEM((DEVICES, LANES), i32),
            pltpu.VMEM((64, LANES), f32),
            pltpu.VMEM((1, LANES), f32),
            pltpu.VMEM((1, LANES), f32),
            pltpu.VMEM((K, 8, 8, NBR), f32),
            pltpu.VMEM((8, 8, NBR), f32),
            dma((16,)), dma, dma((16,)), dma((4,)), dma,
            pltpu.VMEM((NBLK, 8, NBR + LANES), f32),
            pltpu.VMEM((NBLK, 8, NBR), f32),
            pltpu.VMEM((NBLK, 8, NBR), f32),
            pltpu.VMEM((DEVICES, LANES), f32),
            pltpu.VMEM((2, DEVICES, LANES), f32),
            pltpu.VMEM((DEVICES, LANES), i32),
            pltpu.VMEM((DEVICES, LANES), i32),
            pltpu.VMEM((1, LANES), f32),
            pltpu.VMEM((2, NGRP, 1, LANES), f32),
            pltpu.VMEM((1, LANES), f32),
            pltpu.VMEM((DEVICES, LANES), f32),
            pltpu.VMEM((KRYLOV + 1, 8, NBR), f32),
            pltpu.VMEM((KRYLOV, 8, NBR), f32),
            pltpu.VMEM((KRYLOV + 1, 8, LANES), f32),
            pltpu.VMEM((KRYLOV, 8, LANES), f32),
            pltpu.VMEM((8, NBR), i32),
            pltpu.VMEM((1, NBR), i32),
            pltpu.VMEM((16, 8, LANES), f32),
            dma, dma, dma, dma, dma((3,)), dma, dma, dma, dma((3,)), dma((3,)),
        ],
        compiler_params=pltpu.CompilerParams(collective_id=0, has_side_effects=True, vmem_limit_bytes=48 * 1024 * 1024),
    )(stamps, stamp_target.reshape(DEVICES, LANES), pair_counts, conductance, newton_residual, block_cols)


def solution(mesh):
    return jax.shard_map(
        local,
        mesh=mesh,
        in_specs=(
            P(AXES, None, None, None),
            P(AXES, None, None),
            P(AXES, None),
            P(None, AXES),
            P(None, AXES),
            P(None, AXES),
        ),
        out_specs=(P(None, AXES), P(None, None, None, AXES), P(None, AXES)),
        check_vma=False,
    )
```

```python
import functools
import jax
import jax.numpy as jnp
from jax import lax
from jax.experimental import pallas as pl
from jax.experimental.pallas import tpu as pltpu
from jax.sharding import PartitionSpec as P

K = 16
KRYLOV = 5
NBR = 256
NGRP = 8
NBLK = 16
DEVICES = 128
LANES = 128
FRONT = 32
EPS = 1e-06
MESH = pl.DeviceIdType.MESH
AXES = ("grp", "blk")


def bf(x):
    return x.astype(jnp.float32).astype(jnp.bfloat16)


def iota(shape, dim):
    return lax.broadcasted_iota(jnp.int32, shape, dim)


def lane_pick(table, index):
    return jnp.take_along_axis(table, index, axis=1, mode="promise_in_bounds")


def fold_rows(parts):
    row = iota(parts[0].shape, 0)
    step = 1
    while len(parts) > 1:
        even = (row & step) == 0
        merged = []
        for first, second in zip(parts[0::2], parts[1::2]):
            kept = jnp.where(even, first, second)
            moved = jnp.where(even, second, first)
            merged.append(kept + pltpu.roll(moved, step, 0))
        parts = merged
        step *= 2
    return parts[0]


def block_mul(blocks, vector):
    return fold_rows([blocks[a] * vector for a in range(8)])


def small_solve(gram, scales):
    inv = [1.0 / s for s in scales] + [1.0]
    sc = list(scales) + [1.0]
    n = KRYLOV + 1
    g = [[None] * n for _ in range(n)]
    for l in range(n):
        for m in range(l + 1):
            val = gram[l][m] * sc[l] * sc[m]
            g[l][m] = val
            g[m][l] = val
    beta = jnp.sqrt(gram[0][0] + EPS)
    basis = [[inv[0] / beta]]
    hess = []
    for j in range(KRYLOV):
        b = basis[j]
        w = [None] * (j + 2)
        for l in range(j + 1):
            w[l] = b[l] if w[l] is None else w[l] + b[l]
            w[l + 1] = b[l] * inv[l + 1]
        gw = []
        for l in range(j + 2):
            t = g[l][0] * w[0]
            for m in range(1, j + 2):
                t = t + g[l][m] * w[m]
            gw.append(t)
        column = []
        for i in range(j + 1):
            t = basis[i][0] * gw[0]
            for l in range(1, i + 1):
                t = t + basis[i][l] * gw[l]
            column.append(t)
        for i in range(j + 1):
            for l in range(i + 1):
                w[l] = w[l] - column[i] * basis[i][l]
        sq = None
        for l in range(j + 2):
            t = g[l][0] * w[0]
            for m in range(1, j + 2):
                t = t + g[l][m] * w[m]
            sq = t * w[l] if sq is None else sq + t * w[l]
        length = jnp.sqrt(jnp.maximum(sq, 0.0) + EPS)
        column.append(length)
        hess.append(column)
        scale = 1.0 / length
        basis.append([x * scale for x in w])
    work = [[None] * KRYLOV for _ in range(KRYLOV)]
    for p in range(KRYLOV):
        for q in range(p + 1):
            t = hess[p][0] * hess[q][0]
            for i in range(1, q + 2):
                t = t + hess[p][i] * hess[q][i]
            work[p][q] = t
            work[q][p] = t
    vec = [beta * hess[p][0] for p in range(KRYLOV)]
    for p in range(KRYLOV):
        scale = 1.0 / work[p][p]
        top = [x * scale for x in work[p]]
        tv = vec[p] * scale
        for q in range(KRYLOV):
            if q == p:
                continue
            f = work[q][p]
            work[q] = [x - f * y for x, y in zip(work[q], top)]
            vec[q] = vec[q] - f * tv
        work[p] = top
        vec[p] = tv
    out = []
    for l in range(KRYLOV):
        t = None
        for j in range(l, KRYLOV):
            x = vec[j] * basis[j][l]
            t = x if t is None else t + x
        out.append(t * sc[l])
    return out


def solver_kernel(stamps, target_in, counts_in, cond_in, res_in, cols_in, upd_out, jac_out, pre_out,
                  target, counts, cond, res, cols, upd, idx_lo, idx_hi, far_lo, far_hi, sem_i, sem_o,
                  stage, sbuf, rbuf_s, trep, cntb, tail, ttail, ttsrc, jac, dinv, sem_h, sem_ss, sem_rs, sem_t, sem_j,
                  buf_a, buf_b, buf_c, fsrc, fbuf, req_src, req, nsrc, nbuf, rsrc, rbuf,
                  us, ss, gp, sig, pidx, lst,
                  sem_sa, sem_sb, sem_sc, sem_sf, sem_sn, sem_ra, sem_rb, sem_rc, sem_rf, sem_rn):
    g, i = lax.axis_index("grp"), lax.axis_index("blk")
    me = g * NBLK + i

    def mate(o):
        return (g, (i + o) & (NBLK - 1))

    def peer(o):
        return ((g + o) & (NGRP - 1), i)

    def far_dev(t):
        return (g + 1 + t // NBLK) & (NGRP - 1), (i + t) & (NBLK - 1)

    barrier = pltpu.get_barrier_semaphore()

    def farthest_first(t):
        low = t & 37
        return me ^ (((low ^ 37) << 1) | (low ^ ((t >> 1) & 37)) | (~t & 16))

    def chunk_at(t):
        low = (t >> 2) & 1
        return my_chunk ^ (((low ^ 1) << 3) | ((low ^ (t >> 3)) << 2) | (~t & 3))

    def greet(t, c):
        d = farthest_first(t)
        pl.semaphore_signal(barrier, inc=1, device_id=(d // NBLK, d & (NBLK - 1)), device_id_type=MESH)
        return c

    lax.fori_loop(0, DEVICES - 1, greet, 0)

    my_chunk = me // 8

    def load(t):
        first = pl.multiple_of(((my_chunk + t) & 15) * 8, 8)
        return pltpu.make_async_copy(stamps.at[0, pl.ds(first, 8)], stage.at[pl.ds(first, 8)], sem_h.at[t])

    def start_load(t, c):
        load(t).start()
        return c

    reads = [
        pltpu.make_async_copy(src, dst, sem_i.at[n])
        for n, (src, dst) in enumerate(
            [(cols_in, cols), (target_in, target), (counts_in, counts), (cond_in, cond), (res_in, res)])
    ]
    for read in reads:
        read.start()
    lax.fori_loop(0, 16, start_load, 0)
    jac[...] = jnp.zeros_like(jac)
    us[...] = jnp.zeros_like(us)
    for read in reads:
        read.wait()
    us[0] = -res[...]

    owner_row = iota((DEVICES, NBR), 0)
    upper = bf(iota((NBR, NBR), 0) < iota((NBR, NBR), 1))
    before = jnp.zeros((DEVICES, 1), jnp.float32)
    wanted = jnp.zeros((DEVICES, LANES), jnp.float32)
    listed = jnp.zeros((8, NBR), jnp.float32)
    nt = (((1,), (1,)), ((), ()))
    for k in range(8):
        col = cols[8 + k : 9 + k, :]
        owner = lax.shift_right_logical(col, 8)
        row = col & 255
        hit = owner_row == owner
        one = jnp.where(hit, 1.0, 0.0)
        ahead = jnp.dot(one.astype(jnp.bfloat16), upper, preferred_element_type=jnp.float32) + before
        rank = jnp.sum(jnp.where(hit, ahead, 0.0), axis=0, keepdims=True).astype(jnp.int32)
        before = before + jnp.sum(one, axis=1, keepdims=True)
        place = owner * 16 + rank
        pidx[k : k + 1, :] = place
        rowf = row.astype(jnp.float32)
        ranked = jnp.where((owner_row & 15) == rank, rowf, 0.0).astype(jnp.bfloat16)
        wanted = wanted + lax.dot_general(one.astype(jnp.bfloat16), ranked, nt, preferred_element_type=jnp.float32)
        mine = bf(iota((NBR, NBR), 0) == place - g * NBR)
        rows8 = jnp.broadcast_to(rowf, (8, NBR)).astype(jnp.bfloat16)
        listed = listed + lax.dot_general(rows8, mine, nt, preferred_element_type=jnp.float32)
    req_src[...] = wanted.astype(jnp.int32)
    lst[...] = (lax.shift_right_logical(iota((8, NBR), 1), 4) * NBR + listed.astype(jnp.int32))[0:1]

    for q in range(16):
        half = slice(q % 2 * LANES, (q % 2 + 1) * LANES)
        if q < 14:
            idx = cols[1 + q // 2 : 2 + q // 2, half] - g * (NBLK * NBR)
        else:
            idx = lst[:, half]
        idx = jnp.broadcast_to(idx, (8, LANES))
        idx_lo[q] = idx & 127
        idx_hi[q] = lax.shift_right_logical(idx, 7)
        idx = jnp.broadcast_to(pidx[q // 2 : q // 2 + 1, half], (8, LANES))
        far_lo[q] = idx & 127
        far_hi[q] = lax.shift_right_logical(idx, 7)

    lane_big = iota((DEVICES, LANES), 1)
    row_big = iota((DEVICES, LANES), 0)
    count = jnp.sum(jnp.where(lane_big == row_big, counts[...], 0), axis=1, keepdims=True)
    count = jnp.broadcast_to(count, (DEVICES, LANES))
    cntb[...] = count
    tgt = jnp.where((lane_big < count) & (row_big != me), target[...], -1)
    trep[...] = lane_pick(tgt, lane_big & (FRONT - 1)).astype(jnp.float32)
    nxt = (me + 1) & (DEVICES - 1)
    lane1 = iota((1, LANES), 1)
    ttsrc[...] = jnp.where((lane1 >= FRONT) & (lane1 < cntb[pl.ds(nxt, 1), :]), target[pl.ds(nxt, 1), :], -1).astype(jnp.float32)
    own_target = jnp.where(lane1 < cntb[pl.ds(me, 1), :], target[pl.ds(me, 1), :], -1)
    quarter = lax.shift_right_logical(iota((16, LANES), 1), 5)

    def pack(t, c):
        load(t).wait()
        first = pl.multiple_of(((my_chunk + t) & 15) * 8, 8)
        rows = trep[pl.ds(first, 8), :]
        for e in range(8):
            x = stage[first + e, 0:16, :]
            for q in range(1, 4):
                x = jnp.where(quarter == q, pltpu.roll(stage[first + e, 16 * q : 16 * q + 16, :], 32 * q, 1), x)
            sbuf[first + e, 0:16, :] = x
            sbuf[first + e, 16:17, :] = rows[e : e + 1]
        return c

    lax.fori_loop(0, 16, pack, 0)
    rbuf_s[me] = sbuf[me]
    own_first = pl.multiple_of(my_chunk * 8, 8)
    pl.semaphore_wait(barrier, DEVICES - 1)

    tail_dev = (nxt // NBLK, nxt & (NBLK - 1))
    tail_copy = pltpu.make_async_remote_copy(
        src_ref=stage.at[nxt], dst_ref=tail, send_sem=sem_t.at[0], recv_sem=sem_t.at[1], device_id=tail_dev, device_id_type=MESH)
    tail_copy.start()
    ttail_copy = pltpu.make_async_remote_copy(
        src_ref=ttsrc, dst_ref=ttail, send_sem=sem_t.at[2], recv_sem=sem_t.at[3], device_id=tail_dev, device_id_type=MESH)
    ttail_copy.start()

    def stamp_copy(d):
        return pltpu.make_async_remote_copy(
            src_ref=sbuf.at[d, pl.ds(0, 17)], dst_ref=rbuf_s.at[me, pl.ds(0, 17)], send_sem=sem_ss, recv_sem=sem_rs.at[my_chunk],
            device_id=(d // NBLK, d & (NBLK - 1)), device_id_type=MESH)

    in_chunk = (6, 2, 7, 5, 1, 3, 4, 0)

    def send_chunk(t, c):
        first = chunk_at(t) * 8
        for e in in_chunk:
            stamp_copy(first + ((me ^ e) & 7)).start()
        return c

    lax.fori_loop(0, 15, send_chunk, 0)
    for e in in_chunk[:7]:
        stamp_copy(own_first + ((me ^ e) & 7)).start()

    def ask(t, c):
        dg, di = far_dev(t)
        d = dg * NBLK + di
        pltpu.make_async_remote_copy(
            src_ref=req_src.at[pl.ds(d, 1)], dst_ref=req.at[pl.ds(me, 1)], send_sem=sem_sn.at[2], recv_sem=sem_rn.at[2],
            device_id=(dg, di), device_id_type=MESH).start()
        return c

    lax.fori_loop(0, 112, ask, 0)
    rsrc[...] = jnp.zeros_like(rsrc)

    def whole(ref, rows, send, recv):
        return pltpu.make_async_remote_copy(
            src_ref=ref.at[pl.ds(0, rows)], dst_ref=ref.at[pl.ds(0, rows)], send_sem=send, recv_sem=recv,
            device_id=mate(1), device_id_type=MESH)

    node = iota((NBR, NBR), 0)

    def add_slots(values, goal):
        slot_k = lax.shift_right_arithmetic(goal, 8)
        values = jnp.where(goal >= 0, values, 0.0)
        high = values.astype(jnp.bfloat16)
        low = (values - high.astype(jnp.float32)).astype(jnp.bfloat16)
        both = jnp.concatenate([high, low], axis=1)
        there = bf(node == (goal & 255))
        there = jnp.concatenate([there, there], axis=1)
        twice = jnp.concatenate([slot_k, slot_k], axis=1)
        for k0 in range(0, K, 4):
            rows = [both * bf(jnp.broadcast_to(twice == k0 + k, (64, 2 * NBR))) for k in range(4)]
            part = lax.dot_general(jnp.concatenate(rows, axis=0), there, nt, preferred_element_type=jnp.float32)
            jac[k0 : k0 + 4] = jac[k0 : k0 + 4] + part.reshape(4, 8, 8, NBR)

    def add_chunk(first):
        wide, goals = [], []
        for tile in range(2):
            blocks = [rbuf_s[first + 4 * tile + s, 0:16, :] for s in range(4)]
            parts = []
            for q in range(4):
                x = None
                for s in range(4):
                    y = blocks[s] if s == q else pltpu.roll(blocks[s], (s - q) * 32 % LANES, 1)
                    x = y if x is None else jnp.where(quarter == s, y, x)
                parts.append(x)
            wide.append(jnp.concatenate(parts, axis=0))
            x = rbuf_s[first + 4 * tile, 16:17, :]
            for s in range(1, 4):
                x = jnp.where(quarter[0:1] == s, rbuf_s[first + 4 * tile + s, 16:17, :], x)
            goals.append(x.astype(jnp.int32))
        add_slots(jnp.concatenate(wide, axis=1), jnp.concatenate(goals, axis=1))

    def chunk_wait(first, count, sem):
        return pltpu.make_async_remote_copy(
            src_ref=sbuf.at[pl.ds(0, count), pl.ds(0, 17)], dst_ref=rbuf_s.at[pl.ds(0, count), pl.ds(0, 17)],
            send_sem=sem_ss, recv_sem=sem, device_id=mate(1), device_id_type=MESH)

    tail_copy.wait_recv()
    ttail_copy.wait_recv()
    add_slots(
        jnp.concatenate([stage[me], tail[...]], axis=1),
        jnp.concatenate([own_target, ttail[...].astype(jnp.int32)], axis=1))
    def take_chunk(t, c):
        chunk = chunk_at(t)
        first = pl.multiple_of(chunk * 8, 8)
        chunk_wait(first, 8, sem_rs.at[chunk]).wait_recv()
        add_chunk(first)
        return c

    lax.fori_loop(0, 15, take_chunk, 0)
    chunk_wait(own_first, 7, sem_rs.at[my_chunk]).wait_recv()
    add_chunk(own_first)
    sub8 = iota((8, NBR), 0)
    for a in range(8):
        jac[0, a] = jac[0, a] + jnp.where(sub8 == a, jnp.broadcast_to(cond[a : a + 1, :], (8, NBR)), 0.0)
    jac_copy = pltpu.make_async_copy(jac, jac_out, sem_j)
    jac_copy.start()

    work = [jac[0, a] for a in range(8)]
    inverse = [jnp.where(sub8 == a, 1.0, 0.0) for a in range(8)]
    for p in range(8):
        scale = 1.0 / work[p][p : p + 1, :]
        top_w, top_i = work[p] * scale, inverse[p] * scale
        for a in range(8):
            if a != p:
                factor = work[a][p : p + 1, :]
                work[a] = work[a] - factor * top_w
                inverse[a] = inverse[a] - factor * top_i
        work[p], inverse[p] = top_w, top_i
    for a in range(8):
        dinv[a] = inverse[a]
    chunk_wait(own_first, 127, sem_ss).wait_send()
    tail_copy.wait_send()
    ttail_copy.wait_send()
    asked = whole(req, 112, sem_sn.at[2], sem_rn.at[2])
    asked.wait_recv()
    asked.wait_send()

    y, z_at = i // 4, i & 3
    by_hops = [[] for _ in range(5)]
    for oy in range(4):
        for oz in range(4):
            by_hops[min(oy, 4 - oy) + min(oz, 4 - oz)].append((oy, oz))

    def spread(buf, send, recv):
        for hops in (4, 3, 2, 1):
            for oy, oz in by_hops[hops]:
                to = ((y + oy) & 3) * 4 + ((z_at + oz) & 3)
                pltpu.make_async_remote_copy(
                    src_ref=buf.at[i], dst_ref=buf.at[i], send_sem=send, recv_sem=recv.at[hops],
                    device_id=(g, to), device_id_type=MESH).start()

    def sent(buf, send, recv):
        whole(buf, 15, send, recv.at[0]).wait_send()

    def near_pick(buf, send, recv):
        acc = [jnp.zeros((8, LANES), jnp.float32)] * 16
        for part in ((0, 1, 2, 3), (4,)):
            tables = []
            for hops in part:
                if hops:
                    whole(buf, len(by_hops[hops]), send, recv.at[hops]).wait_recv()
                for oy, oz in by_hops[hops]:
                    tables.append(((y - oy) & 3) * 4 + ((z_at - oz) & 3))
            for q in range(16):
                lo, hi, x = idx_lo[q], idx_hi[q], acc[q]
                for s in tables:
                    for h in range(2):
                        x = jnp.where(hi == 2 * s + h, lane_pick(buf[s, :, h * LANES : (h + 1) * LANES], lo), x)
                acc[q] = x
        return acc

    def add_slot(acc, k, picked):
        return [x + jac[k, a] * picked for a, x in enumerate(acc)]

    def joined(first, second):
        return jnp.concatenate([first, second], axis=1)

    def near_couple(buf, send, recv):
        picked = near_pick(buf, send, recv)
        acc = [jnp.zeros((8, NBR), jnp.float32)] * 8
        for k in range(7):
            acc = add_slot(acc, 1 + k, joined(picked[2 * k], picked[2 * k + 1]))
        for k in range(8):
            got = []
            for h in range(2):
                x = jnp.zeros((8, LANES), jnp.float32)
                for v in range(2):
                    x = jnp.where(far_hi[2 * k + h] == 2 * g + v, lane_pick(picked[14 + v], far_lo[2 * k + h]), x)
                got.append(x)
            acc = add_slot(acc, 8 + k, joined(*got))
        return fold_rows(acc)

    lane16 = iota((8, LANES), 1) & 15
    lane_group = lax.shift_right_logical(iota((8, LANES), 1), 4)
    turn = iota((8, LANES), 0) * 16 + lane16
    x_at, core = g // 2, g & 1
    far_groups = [[(0, 1)], [(1, 0), (1, 1), (3, 0), (3, 1)], [(2, 0), (2, 1)]]

    def step(j, carry):
        slot = j & 1
        u = us[j]
        z = block_mul(dinv, u)
        buf_a[i, :, 0:NBR] = z
        sq = u * u
        buf_a[i, :, NBR : NBR + LANES] = sq[:, :LANES] + sq[:, LANES:]
        spread(buf_a, sem_sa, sem_ra)
        dots = []
        for l in range(6):
            t = u * us[l]
            dots.append(t[:, :LANES] + t[:, LANES:])
        zero = jnp.zeros((8, LANES), jnp.float32)
        gp[j] = fold_rows(dots + [zero, zero])
        z = block_mul(dinv, u - near_couple(buf_a, sem_sa, sem_ra))
        buf_b[i] = z
        spread(buf_b, sem_sb, sem_rb)
        nsum = buf_a[0, :, NBR : NBR + LANES]
        for s in range(1, NBLK):
            nsum = nsum + buf_a[s, :, NBR : NBR + LANES]
        nrow = jnp.sum(nsum, axis=0, keepdims=True)
        nsrc[...] = nrow
        for o in range(1, NGRP):
            pltpu.make_async_remote_copy(
                src_ref=nsrc, dst_ref=nbuf.at[slot, g], send_sem=sem_sn.at[slot], recv_sem=sem_rn.at[slot],
                device_id=peer(o), device_id_type=MESH).start()
        nbuf[slot, g] = nrow
        sent(buf_a, sem_sa, sem_ra)
        z = block_mul(dinv, u - near_couple(buf_b, sem_sb, sem_rb))
        buf_c[i] = z

        def far_send(dx, dc, half):
            dg = ((x_at + dx) & 3) * 2 + (core ^ dc)
            first = pl.multiple_of(dg * NBLK + half * 8, 8)
            idx = req[pl.ds(first, 8), :]
            lo, hi = idx & 127, lax.shift_right_logical(idx, 7)
            out = jnp.zeros((8, LANES), jnp.float32)
            for b in range(8):
                for h in range(2):
                    table = jnp.broadcast_to(z[b : b + 1, h * LANES : (h + 1) * LANES], (8, LANES))
                    out = jnp.where((hi == h) & (lane_group == b), lane_pick(table, lo), out)
            fsrc[pl.ds(first, 8), :] = out
            for d in range(8):
                pltpu.make_async_remote_copy(
                    src_ref=fsrc.at[pl.ds(first + d, 1)], dst_ref=fbuf.at[slot, pl.ds(me, 1)],
                    send_sem=sem_sf, recv_sem=sem_rf.at[slot, {0: 0, 1: 1, 3: 1, 2: 2}[dx]],
                    device_id=(dg, half * 8 + d), device_id_type=MESH).start()

        for dx, dc in far_groups[2]:
            for half in range(2):
                far_send(dx, dc, half)
        spread(buf_c, sem_sc, sem_rc)
        for dx, dc in far_groups[1] + far_groups[0]:
            for half in range(2):
                far_send(dx, dc, half)
        sent(buf_b, sem_sb, sem_rb)
        ss[j] = z
        acc = [jac[0, a] * z for a in range(8)]
        picked = near_pick(buf_c, sem_sc, sem_rc)
        for k in range(7):
            acc = add_slot(acc, 1 + k, joined(picked[2 * k], picked[2 * k + 1]))
        got = [jnp.zeros((8, LANES), jnp.float32)] * 16

        def place_far(tables):
            for q in range(16):
                lo, hi, x = far_lo[q], far_hi[q], got[q]
                for at, table in tables:
                    x = jnp.where(hi == at, lane_pick(table, lo), x)
                got[q] = x

        place_far([(2 * g + v, picked[14 + v]) for v in range(2)])
        sent(buf_c, sem_sc, sem_rc)

        def far_part(count, cls):
            return pltpu.make_async_remote_copy(
                src_ref=fsrc.at[pl.ds(0, count)], dst_ref=fbuf.at[slot, pl.ds(0, count)], send_sem=sem_sf,
                recv_sem=sem_rf.at[slot, cls], device_id=mate(1), device_id_type=MESH)

        for cls, groups in enumerate(far_groups):
            far_part(16 * len(groups), cls).wait_recv()
            tables = []
            for dx, dc in groups:
                dg = ((x_at + dx) & 3) * 2 + (core ^ dc)
                for half in range(2):
                    rows = fbuf[slot, pl.ds(pl.multiple_of(dg * NBLK + half * 8, 8), 8), :]
                    table = jnp.zeros((8, LANES), jnp.float32)
                    for o in range(8):
                        table = jnp.where(lane_group == o, lane_pick(jnp.broadcast_to(rows[o : o + 1], (8, LANES)), turn), table)
                    tables.append((2 * dg + half, table))
            place_far(tables)
        for k in range(8):
            acc = add_slot(acc, 8 + k, joined(got[2 * k], got[2 * k + 1]))
        image = fold_rows(acc)
        done_n = pltpu.make_async_remote_copy(
            src_ref=nbuf.at[slot, pl.ds(0, 7)], dst_ref=nbuf.at[slot, pl.ds(0, 7)], send_sem=sem_sn.at[slot], recv_sem=sem_rn.at[slot],
            device_id=mate(1), device_id_type=MESH)
        done_n.wait_recv()
        total = nbuf[slot, 0]
        for s in range(1, NGRP):
            total = total + nbuf[slot, s]
        scale = lax.rsqrt(jnp.maximum(jnp.sum(total, axis=1, keepdims=True), 1e-12))
        sig[j] = jnp.broadcast_to(scale, (8, LANES))
        us[j + 1] = (image - u) * scale
        done_n.wait_send()
        far_part(112, 0).wait_send()
        return carry

    lax.fori_loop(0, KRYLOV, step, 0)

    pre_copy = pltpu.make_async_copy(ss.at[0], pre_out, sem_o.at[0])
    pre_copy.start()
    u = us[KRYLOV]
    dots = []
    for l in range(6):
        t = u * us[l]
        dots.append(t[:, :LANES] + t[:, LANES:])
    zero = jnp.zeros((8, LANES), jnp.float32)
    gp[KRYLOV] = fold_rows(dots + [zero, zero])
    row = jnp.zeros((1, LANES), jnp.float32)
    lane = iota((8, LANES), 1)
    sub = iota((8, LANES), 0)
    for j in range(6):
        s = jnp.sum(gp[j], axis=1, keepdims=True)
        row = row + jnp.sum(jnp.where(lane == 8 * j + sub, s, 0.0), axis=0, keepdims=True)
    rsrc[...] = row

    def tell(t, c):
        d = farthest_first(t)
        pltpu.make_async_remote_copy(
            src_ref=rsrc, dst_ref=rbuf.at[pl.ds(me, 1)], send_sem=sem_sf, recv_sem=sem_rf.at[2, 0],
            device_id=(d // NBLK, d & (NBLK - 1)), device_id_type=MESH).start()
        return c

    lax.fori_loop(0, DEVICES - 1, tell, 0)
    rbuf[pl.ds(me, 1), :] = row
    done = whole(rbuf, 127, sem_sf, sem_rf.at[2, 0])
    done.wait_recv()
    done.wait_send()
    total = rbuf[0:8, :]
    for q in range(1, 16):
        total = total + rbuf[8 * q : 8 * q + 8, :]
    total = jnp.sum(total, axis=0, keepdims=True)
    gram = [[jnp.broadcast_to(total[:, 8 * j + l : 8 * j + l + 1], (8, LANES)) for l in range(j + 1)] for j in range(6)]
    weights = small_solve(gram, [sig[j] for j in range(KRYLOV)])
    for h in range(2):
        part = slice(h * LANES, (h + 1) * LANES)
        x = weights[0] * ss[0, :, part]
        for l in range(1, KRYLOV):
            x = x + weights[l] * ss[l, :, part]
        upd[:, part] = x
    upd_copy = pltpu.make_async_copy(upd, upd_out, sem_o.at[1])
    upd_copy.start()
    jac_copy.wait()
    pre_copy.wait()
    upd_copy.wait()


def hand_on(upd_in, jac_in, pre_in, upd, jac, pre, upd_v, jac_v, pre_v, sem_in, sem_out):
    parts = [(upd_in, upd_v, upd), (pre_in, pre_v, pre)]
    for n in range(0, K, 4):
        part = pl.ds(n, 4)
        parts.append((jac_in.at[part], jac_v.at[part], jac.at[part]))
    reads = [pltpu.make_async_copy(src, mid, sem_in.at[n]) for n, (src, mid, _) in enumerate(parts)]
    writes = [pltpu.make_async_copy(mid, dst, sem_out.at[n]) for n, (_, mid, dst) in enumerate(parts)]
    for read in reads:
        read.start()
    for read, write in zip(reads, writes):
        read.wait()
        write.start()
    for write in writes:
        write.wait()


def local(stamps, stamp_target, pair_counts, conductance, block_cols, newton_residual):
    hbm = pl.BlockSpec(memory_space=pl.ANY)
    f32, i32 = jnp.float32, jnp.int32
    dma = pltpu.SemaphoreType.DMA
    shapes = (
            jax.ShapeDtypeStruct((8, NBR), f32),
            jax.ShapeDtypeStruct((K, 8, 8, NBR), f32),
            jax.ShapeDtypeStruct((8, NBR), f32),
    )
    results = pl.pallas_call(
        solver_kernel,
        out_shape=shapes,
        in_specs=[hbm] * 6,
        out_specs=(hbm, hbm, hbm),
        scratch_shapes=[
            pltpu.VMEM((DEVICES, LANES), i32),
            pltpu.VMEM((1, LANES), i32),
            pltpu.VMEM((8, NBR), f32),
            pltpu.VMEM((8, NBR), f32),
            pltpu.VMEM((K, NBR), i32),
            pltpu.VMEM((8, NBR), f32),
            pltpu.VMEM((16, 8, LANES), i32),
            pltpu.VMEM((16, 8, LANES), i32),
            pltpu.VMEM((16, 8, LANES), i32),
            pltpu.VMEM((16, 8, LANES), i32),
            dma((5,)), dma((2,)),
            pltpu.VMEM((DEVICES, 64, LANES), f32),
            pltpu.VMEM((DEVICES, 24, LANES), f32),
            pltpu.VMEM((DEVICES, 24, LANES), f32),
            pltpu.VMEM((DEVICES, LANES), f32),
            pltpu.VMEM((DEVICES, LANES), i32),
            pltpu.VMEM((64, LANES), f32),
            pltpu.VMEM((1, LANES), f32),
            pltpu.VMEM((1, LANES), f32),
            pltpu.VMEM((K, 8, 8, NBR), f32),
            pltpu.VMEM((8, 8, NBR), f32),
            dma((16,)), dma, dma((16,)), dma((4,)), dma,
            pltpu.VMEM((NBLK, 8, NBR + LANES), f32),
            pltpu.VMEM((NBLK, 8, NBR), f32),
            pltpu.VMEM((NBLK, 8, NBR), f32),
            pltpu.VMEM((DEVICES, LANES), f32),
            pltpu.VMEM((2, DEVICES, LANES), f32),
            pltpu.VMEM((DEVICES, LANES), i32),
            pltpu.VMEM((DEVICES, LANES), i32),
            pltpu.VMEM((1, LANES), f32),
            pltpu.VMEM((2, NGRP, 1, LANES), f32),
            pltpu.VMEM((1, LANES), f32),
            pltpu.VMEM((DEVICES, LANES), f32),
            pltpu.VMEM((KRYLOV + 1, 8, NBR), f32),
            pltpu.VMEM((KRYLOV, 8, NBR), f32),
            pltpu.VMEM((KRYLOV + 1, 8, LANES), f32),
            pltpu.VMEM((KRYLOV, 8, LANES), f32),
            pltpu.VMEM((8, NBR), i32),
            pltpu.VMEM((1, NBR), i32),
            dma, dma, dma, dma, dma((3,)), dma((5,)), dma((5,)), dma((5,)), dma((3, 3)), dma((3,)),
        ],
        compiler_params=pltpu.CompilerParams(collective_id=0, has_side_effects=True, vmem_limit_bytes=62 * 1024 * 1024),
    )(stamps, stamp_target.reshape(DEVICES, LANES), pair_counts, conductance, newton_residual, block_cols)
    return pl.pallas_call(
        hand_on,
        out_shape=shapes,
        in_specs=[hbm] * 3,
        out_specs=(hbm, hbm, hbm),
        scratch_shapes=[
            pltpu.VMEM((8, NBR), f32), pltpu.VMEM((K, 8, 8, NBR), f32), pltpu.VMEM((8, NBR), f32), dma((6,)), dma((6,)),
        ],
        compiler_params=pltpu.CompilerParams(vmem_limit_bytes=62 * 1024 * 1024),
    )(*results)


def solution(mesh):
    return jax.shard_map(
        local,
        mesh=mesh,
        in_specs=(
            P(AXES, None, None, None),
            P(AXES, None, None),
            P(AXES, None),
            P(None, AXES),
            P(None, AXES),
            P(None, AXES),
        ),
        out_specs=(P(None, AXES), P(None, None, None, AXES), P(None, AXES)),
        check_vma=False,
    )
```

```python
import functools
import jax
import jax.numpy as jnp
from jax import lax
from jax.experimental import pallas as pl
from jax.experimental.pallas import tpu as pltpu
from jax.sharding import PartitionSpec as P

K = 16
KRYLOV = 5
NBR = 256
NGRP = 8
NBLK = 16
DEVICES = 128
LANES = 128
FRONT = 32
EPS = 1e-06
MESH = pl.DeviceIdType.MESH
AXES = ("grp", "blk")


def bf(x):
    return x.astype(jnp.float32).astype(jnp.bfloat16)


def iota(shape, dim):
    return lax.broadcasted_iota(jnp.int32, shape, dim)


def lane_pick(table, index):
    return jnp.take_along_axis(table, index, axis=1, mode="promise_in_bounds")


def fold_rows(parts):
    row = iota(parts[0].shape, 0)
    step = 1
    while len(parts) > 1:
        even = (row & step) == 0
        merged = []
        for first, second in zip(parts[0::2], parts[1::2]):
            kept = jnp.where(even, first, second)
            moved = jnp.where(even, second, first)
            merged.append(kept + pltpu.roll(moved, step, 0))
        parts = merged
        step *= 2
    return parts[0]


def block_mul(blocks, vector):
    return fold_rows([blocks[a] * vector for a in range(8)])


def small_solve(gram, scales):
    inv = [1.0 / s for s in scales] + [1.0]
    sc = list(scales) + [1.0]
    n = KRYLOV + 1
    g = [[None] * n for _ in range(n)]
    for l in range(n):
        for m in range(l + 1):
            val = gram[l][m] * sc[l] * sc[m]
            g[l][m] = val
            g[m][l] = val
    beta = jnp.sqrt(gram[0][0] + EPS)
    basis = [[inv[0] / beta]]
    hess = []
    for j in range(KRYLOV):
        b = basis[j]
        w = [None] * (j + 2)
        for l in range(j + 1):
            w[l] = b[l] if w[l] is None else w[l] + b[l]
            w[l + 1] = b[l] * inv[l + 1]
        gw = []
        for l in range(j + 2):
            t = g[l][0] * w[0]
            for m in range(1, j + 2):
                t = t + g[l][m] * w[m]
            gw.append(t)
        column = []
        for i in range(j + 1):
            t = basis[i][0] * gw[0]
            for l in range(1, i + 1):
                t = t + basis[i][l] * gw[l]
            column.append(t)
        for i in range(j + 1):
            for l in range(i + 1):
                w[l] = w[l] - column[i] * basis[i][l]
        sq = None
        for l in range(j + 2):
            t = g[l][0] * w[0]
            for m in range(1, j + 2):
                t = t + g[l][m] * w[m]
            sq = t * w[l] if sq is None else sq + t * w[l]
        length = jnp.sqrt(jnp.maximum(sq, 0.0) + EPS)
        column.append(length)
        hess.append(column)
        scale = 1.0 / length
        basis.append([x * scale for x in w])
    work = [[None] * KRYLOV for _ in range(KRYLOV)]
    for p in range(KRYLOV):
        for q in range(p + 1):
            t = hess[p][0] * hess[q][0]
            for i in range(1, q + 2):
                t = t + hess[p][i] * hess[q][i]
            work[p][q] = t
            work[q][p] = t
    vec = [beta * hess[p][0] for p in range(KRYLOV)]
    for p in range(KRYLOV):
        scale = 1.0 / work[p][p]
        top = [x * scale for x in work[p]]
        tv = vec[p] * scale
        for q in range(KRYLOV):
            if q == p:
                continue
            f = work[q][p]
            work[q] = [x - f * y for x, y in zip(work[q], top)]
            vec[q] = vec[q] - f * tv
        work[p] = top
        vec[p] = tv
    out = []
    for l in range(KRYLOV):
        t = None
        for j in range(l, KRYLOV):
            x = vec[j] * basis[j][l]
            t = x if t is None else t + x
        out.append(t * sc[l])
    return out


def solver_kernel(stamps, target_in, counts_in, cond_in, res_in, cols_in, upd_out, jac_out, pre_out,
                  target, counts, cond, res, cols, upd, idx_lo, idx_hi, far_lo, far_hi, gbuf, sem_g, sem_i, sem_o,
                  stage, sbuf, rbuf_s, trep, cntb, tail, ttail, ttsrc, jac, dinv, sem_h, sem_ss, sem_rs, sem_t, sem_j,
                  buf_a, buf_b, buf_c, fsrc, fbuf, req_src, req, nsrc, nbuf, rsrc, rbuf,
                  us, ss, gp, sig, pidx, lst,
                  sem_sa, sem_sb, sem_sc, sem_sf, sem_sn, sem_ra, sem_rb, sem_rc, sem_rf, sem_rn):
    g, i = lax.axis_index("grp"), lax.axis_index("blk")
    me = g * NBLK + i

    def mate(o):
        return (g, (i + o) & (NBLK - 1))

    def peer(o):
        return ((g + o) & (NGRP - 1), i)

    def far_dev(t):
        return (g + 1 + t // NBLK) & (NGRP - 1), (i + t) & (NBLK - 1)

    barrier = pltpu.get_barrier_semaphore()

    def farthest_first(t):
        low = t & 37
        return me ^ (((low ^ 37) << 1) | (low ^ ((t >> 1) & 37)) | (~t & 16))

    def chunk_at(t):
        low = (t >> 2) & 1
        return my_chunk ^ (((low ^ 1) << 3) | ((low ^ (t >> 3)) << 2) | (~t & 3))

    def greet(t, c):
        d = farthest_first(t)
        pl.semaphore_signal(barrier, inc=1, device_id=(d // NBLK, d & (NBLK - 1)), device_id_type=MESH)
        return c

    lax.fori_loop(0, DEVICES - 1, greet, 0)

    my_chunk = me // 8

    def load(t):
        first = pl.multiple_of(((my_chunk + t) & 15) * 8, 8)
        return pltpu.make_async_copy(stamps.at[0, pl.ds(first, 8)], stage.at[pl.ds(first, 8)], sem_h.at[t])

    def start_load(t, c):
        load(t).start()
        return c

    reads = [
        pltpu.make_async_copy(src, dst, sem_i.at[n])
        for n, (src, dst) in enumerate(
            [(cols_in, cols), (target_in, target), (counts_in, counts), (cond_in, cond), (res_in, res)])
    ]
    for read in reads:
        read.start()
    lax.fori_loop(0, 16, start_load, 0)
    jac[...] = jnp.zeros_like(jac)
    us[...] = jnp.zeros_like(us)
    for read in reads:
        read.wait()
    us[0] = -res[...]

    nt = (((1,), (1,)), ((), ()))
    lane_big = iota((DEVICES, LANES), 1)
    row_big = iota((DEVICES, LANES), 0)
    count = jnp.sum(jnp.where(lane_big == row_big, counts[...], 0), axis=1, keepdims=True)
    count = jnp.broadcast_to(count, (DEVICES, LANES))
    cntb[...] = count
    tgt = jnp.where((lane_big < count) & (row_big != me), target[...], -1)
    trep[...] = lane_pick(tgt, lane_big & (FRONT - 1)).astype(jnp.float32)
    nxt = (me + 1) & (DEVICES - 1)
    lane1 = iota((1, LANES), 1)
    ttsrc[...] = jnp.where((lane1 >= FRONT) & (lane1 < cntb[pl.ds(nxt, 1), :]), target[pl.ds(nxt, 1), :], -1).astype(jnp.float32)
    own_target = jnp.where(lane1 < cntb[pl.ds(me, 1), :], target[pl.ds(me, 1), :], -1)
    quarter = lax.shift_right_logical(iota((16, LANES), 1), 5)

    def pack(t, c):
        load(t).wait()
        first = pl.multiple_of(((my_chunk + t) & 15) * 8, 8)
        rows = trep[pl.ds(first, 8), :]
        for e in range(8):
            x = stage[first + e, 0:16, :]
            for q in range(1, 4):
                x = jnp.where(quarter == q, pltpu.roll(stage[first + e, 16 * q : 16 * q + 16, :], 32 * q, 1), x)
            sbuf[first + e, 0:16, :] = x
            sbuf[first + e, 16:17, :] = rows[e : e + 1]
        return c

    lax.fori_loop(0, 16, pack, 0)
    rbuf_s[me] = sbuf[me]
    own_first = pl.multiple_of(my_chunk * 8, 8)
    pl.semaphore_wait(barrier, DEVICES - 1)

    tail_dev = (nxt // NBLK, nxt & (NBLK - 1))
    tail_copy = pltpu.make_async_remote_copy(
        src_ref=stage.at[nxt], dst_ref=tail, send_sem=sem_t.at[0], recv_sem=sem_t.at[1], device_id=tail_dev, device_id_type=MESH)
    tail_copy.start()
    ttail_copy = pltpu.make_async_remote_copy(
        src_ref=ttsrc, dst_ref=ttail, send_sem=sem_t.at[2], recv_sem=sem_t.at[3], device_id=tail_dev, device_id_type=MESH)
    ttail_copy.start()

    def stamp_copy(d):
        return pltpu.make_async_remote_copy(
            src_ref=sbuf.at[d, pl.ds(0, 17)], dst_ref=rbuf_s.at[me, pl.ds(0, 17)], send_sem=sem_ss, recv_sem=sem_rs.at[my_chunk],
            device_id=(d // NBLK, d & (NBLK - 1)), device_id_type=MESH)

    in_chunk = (6, 2, 7, 5, 1, 3, 4, 0)

    def send_chunk(t, c):
        first = chunk_at(t) * 8
        for e in in_chunk:
            stamp_copy(first + ((me ^ e) & 7)).start()
        return c

    lax.fori_loop(0, 15, send_chunk, 0)
    for e in in_chunk[:7]:
        stamp_copy(own_first + ((me ^ e) & 7)).start()

    owner_row = iota((DEVICES, NBR), 0)
    upper = bf(iota((NBR, NBR), 0) < iota((NBR, NBR), 1))
    before = jnp.zeros((DEVICES, 1), jnp.float32)
    wanted = jnp.zeros((DEVICES, LANES), jnp.float32)
    listed = jnp.zeros((8, NBR), jnp.float32)
    nt = (((1,), (1,)), ((), ()))
    for k in range(8):
        col = cols[8 + k : 9 + k, :]
        owner = lax.shift_right_logical(col, 8)
        row = col & 255
        hit = owner_row == owner
        one = jnp.where(hit, 1.0, 0.0)
        ahead = jnp.dot(one.astype(jnp.bfloat16), upper, preferred_element_type=jnp.float32) + before
        rank = jnp.sum(jnp.where(hit, ahead, 0.0), axis=0, keepdims=True).astype(jnp.int32)
        before = before + jnp.sum(one, axis=1, keepdims=True)
        place = owner * 16 + rank
        pidx[k : k + 1, :] = place
        rowf = row.astype(jnp.float32)
        ranked = jnp.where((owner_row & 15) == rank, rowf, 0.0).astype(jnp.bfloat16)
        wanted = wanted + lax.dot_general(one.astype(jnp.bfloat16), ranked, nt, preferred_element_type=jnp.float32)
        mine = bf(iota((NBR, NBR), 0) == place - g * NBR)
        rows8 = jnp.broadcast_to(rowf, (8, NBR)).astype(jnp.bfloat16)
        listed = listed + lax.dot_general(rows8, mine, nt, preferred_element_type=jnp.float32)
    req_src[...] = wanted.astype(jnp.int32)
    lst[...] = (lax.shift_right_logical(iota((8, NBR), 1), 4) * NBR + listed.astype(jnp.int32))[0:1]

    for q in range(16):
        half = slice(q % 2 * LANES, (q % 2 + 1) * LANES)
        if q < 14:
            idx = cols[1 + q // 2 : 2 + q // 2, half] - g * (NBLK * NBR)
        else:
            idx = lst[:, half]
        idx = jnp.broadcast_to(idx, (8, LANES))
        idx_lo[q] = idx & 127
        idx_hi[q] = lax.shift_right_logical(idx, 7)
        idx = jnp.broadcast_to(pidx[q // 2 : q // 2 + 1, half], (8, LANES))
        far_lo[q] = idx & 127
        far_hi[q] = lax.shift_right_logical(idx, 7)

    def ask(t, c):
        dg, di = far_dev(t)
        d = dg * NBLK + di
        pltpu.make_async_remote_copy(
            src_ref=req_src.at[pl.ds(d, 1)], dst_ref=req.at[pl.ds(me, 1)], send_sem=sem_sn.at[2], recv_sem=sem_rn.at[2],
            device_id=(dg, di), device_id_type=MESH).start()
        return c

    lax.fori_loop(0, 112, ask, 0)
    rsrc[...] = jnp.zeros_like(rsrc)

    def whole(ref, rows, send, recv):
        return pltpu.make_async_remote_copy(
            src_ref=ref.at[pl.ds(0, rows)], dst_ref=ref.at[pl.ds(0, rows)], send_sem=send, recv_sem=recv,
            device_id=mate(1), device_id_type=MESH)

    node = iota((NBR, NBR), 0)

    def add_slots(values, goal):
        slot_k = lax.shift_right_arithmetic(goal, 8)
        values = jnp.where(goal >= 0, values, 0.0)
        high = values.astype(jnp.bfloat16)
        low = (values - high.astype(jnp.float32)).astype(jnp.bfloat16)
        both = jnp.concatenate([high, low], axis=1)
        there = bf(node == (goal & 255))
        there = jnp.concatenate([there, there], axis=1)
        twice = jnp.concatenate([slot_k, slot_k], axis=1)
        for k0 in range(0, K, 4):
            rows = [both * bf(jnp.broadcast_to(twice == k0 + k, (64, 2 * NBR))) for k in range(4)]
            part = lax.dot_general(jnp.concatenate(rows, axis=0), there, nt, preferred_element_type=jnp.float32)
            jac[k0 : k0 + 4] = jac[k0 : k0 + 4] + part.reshape(4, 8, 8, NBR)

    def add_chunk(first):
        wide, goals = [], []
        for tile in range(2):
            blocks = [rbuf_s[first + 4 * tile + s, 0:16, :] for s in range(4)]
            parts = []
            for q in range(4):
                x = None
                for s in range(4):
                    y = blocks[s] if s == q else pltpu.roll(blocks[s], (s - q) * 32 % LANES, 1)
                    x = y if x is None else jnp.where(quarter == s, y, x)
                parts.append(x)
            wide.append(jnp.concatenate(parts, axis=0))
            x = rbuf_s[first + 4 * tile, 16:17, :]
            for s in range(1, 4):
                x = jnp.where(quarter[0:1] == s, rbuf_s[first + 4 * tile + s, 16:17, :], x)
            goals.append(x.astype(jnp.int32))
        add_slots(jnp.concatenate(wide, axis=1), jnp.concatenate(goals, axis=1))

    def chunk_wait(first, count, sem):
        return pltpu.make_async_remote_copy(
            src_ref=sbuf.at[pl.ds(0, count), pl.ds(0, 17)], dst_ref=rbuf_s.at[pl.ds(0, count), pl.ds(0, 17)],
            send_sem=sem_ss, recv_sem=sem, device_id=mate(1), device_id_type=MESH)

    tail_copy.wait_recv()
    ttail_copy.wait_recv()
    add_slots(
        jnp.concatenate([stage[me], tail[...]], axis=1),
        jnp.concatenate([own_target, ttail[...].astype(jnp.int32)], axis=1))
    def take_chunk(t, c):
        chunk = chunk_at(t)
        first = pl.multiple_of(chunk * 8, 8)
        chunk_wait(first, 8, sem_rs.at[chunk]).wait_recv()
        add_chunk(first)
        return c

    lax.fori_loop(0, 15, take_chunk, 0)
    chunk_wait(own_first, 7, sem_rs.at[my_chunk]).wait_recv()
    add_chunk(own_first)
    sub8 = iota((8, NBR), 0)
    for a in range(8):
        jac[0, a] = jac[0, a] + jnp.where(sub8 == a, jnp.broadcast_to(cond[a : a + 1, :], (8, NBR)), 0.0)
    jac_copy = pltpu.make_async_copy(jac, jac_out, sem_j)
    jac_copy.start()

    work = [jac[0, a] for a in range(8)]
    inverse = [jnp.where(sub8 == a, 1.0, 0.0) for a in range(8)]
    for p in range(8):
        scale = 1.0 / work[p][p : p + 1, :]
        top_w, top_i = work[p] * scale, inverse[p] * scale
        for a in range(8):
            if a != p:
                factor = work[a][p : p + 1, :]
                work[a] = work[a] - factor * top_w
                inverse[a] = inverse[a] - factor * top_i
        work[p], inverse[p] = top_w, top_i
    for a in range(8):
        dinv[a] = inverse[a]
    chunk_wait(own_first, 127, sem_ss).wait_send()
    tail_copy.wait_send()
    ttail_copy.wait_send()
    asked = whole(req, 112, sem_sn.at[2], sem_rn.at[2])
    asked.wait_recv()
    asked.wait_send()

    y, z_at = i // 4, i & 3
    by_hops = [[] for _ in range(5)]
    for oy in range(4):
        for oz in range(4):
            by_hops[min(oy, 4 - oy) + min(oz, 4 - oz)].append((oy, oz))

    def spread(buf, send, recv):
        for hops in (4, 3, 2, 1):
            for oy, oz in by_hops[hops]:
                to = ((y + oy) & 3) * 4 + ((z_at + oz) & 3)
                pltpu.make_async_remote_copy(
                    src_ref=buf.at[i], dst_ref=buf.at[i], send_sem=send, recv_sem=recv.at[hops],
                    device_id=(g, to), device_id_type=MESH).start()

    def sent(buf, send, recv):
        whole(buf, 15, send, recv.at[0]).wait_send()

    def near_pick(buf, send, recv):
        acc = [jnp.zeros((8, LANES), jnp.float32)] * 16
        for part in ((0, 1, 2, 3), (4,)):
            tables = []
            for hops in part:
                if hops:
                    whole(buf, len(by_hops[hops]), send, recv.at[hops]).wait_recv()
                for oy, oz in by_hops[hops]:
                    tables.append(((y - oy) & 3) * 4 + ((z_at - oz) & 3))
            for q in range(16):
                lo, hi, x = idx_lo[q], idx_hi[q], acc[q]
                for s in tables:
                    for h in range(2):
                        x = jnp.where(hi == 2 * s + h, lane_pick(buf[s, :, h * LANES : (h + 1) * LANES], lo), x)
                acc[q] = x
        return acc

    def add_slot(acc, k, picked):
        return [x + jac[k, a] * picked for a, x in enumerate(acc)]

    def joined(first, second):
        return jnp.concatenate([first, second], axis=1)

    def near_couple(buf, send, recv):
        picked = near_pick(buf, send, recv)
        acc = [jnp.zeros((8, NBR), jnp.float32)] * 8
        for k in range(7):
            acc = add_slot(acc, 1 + k, joined(picked[2 * k], picked[2 * k + 1]))
        for k in range(8):
            got = []
            for h in range(2):
                x = jnp.zeros((8, LANES), jnp.float32)
                for v in range(2):
                    x = jnp.where(far_hi[2 * k + h] == 2 * g + v, lane_pick(picked[14 + v], far_lo[2 * k + h]), x)
                got.append(x)
            acc = add_slot(acc, 8 + k, joined(*got))
        return fold_rows(acc)

    lane16 = iota((8, LANES), 1) & 15
    lane_group = lax.shift_right_logical(iota((8, LANES), 1), 4)
    turn = iota((8, LANES), 0) * 16 + lane16
    x_at, core = g // 2, g & 1
    far_groups = [[(0, 1)], [(1, 0), (1, 1), (3, 0), (3, 1)], [(2, 0), (2, 1)]]

    def step(j, carry):
        slot = j & 1
        u = us[j]
        z = block_mul(dinv, u)
        buf_a[i] = z
        spread(buf_a, sem_sa, sem_ra)
        sq = u * u
        gbuf[i] = jnp.sum(sq[:, :LANES] + sq[:, LANES:], axis=0, keepdims=True)
        for o in range(1, NBLK):
            pltpu.make_async_remote_copy(
                src_ref=gbuf.at[i], dst_ref=gbuf.at[i], send_sem=sem_g.at[0], recv_sem=sem_g.at[1],
                device_id=mate(o), device_id_type=MESH).start()
        dots = []
        for l in range(6):
            t = u * us[l]
            dots.append(t[:, :LANES] + t[:, LANES:])
        zero = jnp.zeros((8, LANES), jnp.float32)
        gp[j] = fold_rows(dots + [zero, zero])
        z = block_mul(dinv, u - near_couple(buf_a, sem_sa, sem_ra))
        buf_b[i] = z
        spread(buf_b, sem_sb, sem_rb)
        done_g = whole(gbuf, 15, sem_g.at[0], sem_g.at[1])
        done_g.wait_recv()
        nrow = gbuf[0]
        for s in range(1, NBLK):
            nrow = nrow + gbuf[s]
        nsrc[...] = nrow
        for o in range(1, NGRP):
            pltpu.make_async_remote_copy(
                src_ref=nsrc, dst_ref=nbuf.at[slot, g], send_sem=sem_sn.at[slot], recv_sem=sem_rn.at[slot],
                device_id=peer(o), device_id_type=MESH).start()
        nbuf[slot, g] = nrow
        done_g.wait_send()
        sent(buf_a, sem_sa, sem_ra)
        z = block_mul(dinv, u - near_couple(buf_b, sem_sb, sem_rb))
        buf_c[i] = z

        def far_send(dx, dc, half):
            dg = ((x_at + dx) & 3) * 2 + (core ^ dc)
            first = pl.multiple_of(dg * NBLK + half * 8, 8)
            idx = req[pl.ds(first, 8), :]
            lo, hi = idx & 127, lax.shift_right_logical(idx, 7)
            out = jnp.zeros((8, LANES), jnp.float32)
            for b in range(8):
                for h in range(2):
                    table = jnp.broadcast_to(z[b : b + 1, h * LANES : (h + 1) * LANES], (8, LANES))
                    out = jnp.where((hi == h) & (lane_group == b), lane_pick(table, lo), out)
            fsrc[pl.ds(first, 8), :] = out
            for d in range(8):
                pltpu.make_async_remote_copy(
                    src_ref=fsrc.at[pl.ds(first + d, 1)], dst_ref=fbuf.at[slot, pl.ds(me, 1)],
                    send_sem=sem_sf, recv_sem=sem_rf.at[slot, {0: 0, 1: 1, 3: 1, 2: 2}[dx]],
                    device_id=(dg, half * 8 + d), device_id_type=MESH).start()

        for dx, dc in far_groups[2]:
            for half in range(2):
                far_send(dx, dc, half)
        spread(buf_c, sem_sc, sem_rc)
        for dx, dc in far_groups[1] + far_groups[0]:
            for half in range(2):
                far_send(dx, dc, half)
        sent(buf_b, sem_sb, sem_rb)
        ss[j] = z
        acc = [jac[0, a] * z for a in range(8)]
        picked = near_pick(buf_c, sem_sc, sem_rc)
        for k in range(7):
            acc = add_slot(acc, 1 + k, joined(picked[2 * k], picked[2 * k + 1]))
        got = [jnp.zeros((8, LANES), jnp.float32)] * 16

        def place_far(tables):
            for q in range(16):
                lo, hi, x = far_lo[q], far_hi[q], got[q]
                for at, table in tables:
                    x = jnp.where(hi == at, lane_pick(table, lo), x)
                got[q] = x

        place_far([(2 * g + v, picked[14 + v]) for v in range(2)])
        sent(buf_c, sem_sc, sem_rc)

        def far_part(count, cls):
            return pltpu.make_async_remote_copy(
                src_ref=fsrc.at[pl.ds(0, count)], dst_ref=fbuf.at[slot, pl.ds(0, count)], send_sem=sem_sf,
                recv_sem=sem_rf.at[slot, cls], device_id=mate(1), device_id_type=MESH)

        for cls, groups in enumerate(far_groups):
            far_part(16 * len(groups), cls).wait_recv()
            tables = []
            for dx, dc in groups:
                dg = ((x_at + dx) & 3) * 2 + (core ^ dc)
                for half in range(2):
                    rows = fbuf[slot, pl.ds(pl.multiple_of(dg * NBLK + half * 8, 8), 8), :]
                    table = jnp.zeros((8, LANES), jnp.float32)
                    for o in range(8):
                        table = jnp.where(lane_group == o, lane_pick(jnp.broadcast_to(rows[o : o + 1], (8, LANES)), turn), table)
                    tables.append((2 * dg + half, table))
            place_far(tables)
        for k in range(8):
            acc = add_slot(acc, 8 + k, joined(got[2 * k], got[2 * k + 1]))
        image = fold_rows(acc)
        done_n = pltpu.make_async_remote_copy(
            src_ref=nbuf.at[slot, pl.ds(0, 7)], dst_ref=nbuf.at[slot, pl.ds(0, 7)], send_sem=sem_sn.at[slot], recv_sem=sem_rn.at[slot],
            device_id=mate(1), device_id_type=MESH)
        done_n.wait_recv()
        total = nbuf[slot, 0]
        for s in range(1, NGRP):
            total = total + nbuf[slot, s]
        scale = lax.rsqrt(jnp.maximum(jnp.sum(total, axis=1, keepdims=True), 1e-12))
        sig[j] = jnp.broadcast_to(scale, (8, LANES))
        us[j + 1] = (image - u) * scale
        done_n.wait_send()
        far_part(112, 0).wait_send()
        return carry

    lax.fori_loop(0, KRYLOV, step, 0)

    pre_copy = pltpu.make_async_copy(ss.at[0], pre_out, sem_o.at[0])
    pre_copy.start()
    u = us[KRYLOV]
    dots = []
    for l in range(6):
        t = u * us[l]
        dots.append(t[:, :LANES] + t[:, LANES:])
    zero = jnp.zeros((8, LANES), jnp.float32)
    gp[KRYLOV] = fold_rows(dots + [zero, zero])
    row = jnp.zeros((1, LANES), jnp.float32)
    lane = iota((8, LANES), 1)
    sub = iota((8, LANES), 0)
    for j in range(6):
        s = jnp.sum(gp[j], axis=1, keepdims=True)
        row = row + jnp.sum(jnp.where(lane == 8 * j + sub, s, 0.0), axis=0, keepdims=True)
    rsrc[...] = row

    def tell(t, c):
        d = farthest_first(t)
        pltpu.make_async_remote_copy(
            src_ref=rsrc, dst_ref=rbuf.at[pl.ds(me, 1)], send_sem=sem_sf, recv_sem=sem_rf.at[2, 0],
            device_id=(d // NBLK, d & (NBLK - 1)), device_id_type=MESH).start()
        return c

    lax.fori_loop(0, DEVICES - 1, tell, 0)
    rbuf[pl.ds(me, 1), :] = row
    done = whole(rbuf, 127, sem_sf, sem_rf.at[2, 0])
    done.wait_recv()
    done.wait_send()
    total = rbuf[0:8, :]
    for q in range(1, 16):
        total = total + rbuf[8 * q : 8 * q + 8, :]
    total = jnp.sum(total, axis=0, keepdims=True)
    gram = [[jnp.broadcast_to(total[:, 8 * j + l : 8 * j + l + 1], (8, LANES)) for l in range(j + 1)] for j in range(6)]
    weights = small_solve(gram, [sig[j] for j in range(KRYLOV)])
    for h in range(2):
        part = slice(h * LANES, (h + 1) * LANES)
        x = weights[0] * ss[0, :, part]
        for l in range(1, KRYLOV):
            x = x + weights[l] * ss[l, :, part]
        upd[:, part] = x
    upd_copy = pltpu.make_async_copy(upd, upd_out, sem_o.at[1])
    upd_copy.start()
    jac_copy.wait()
    pre_copy.wait()
    upd_copy.wait()


def hand_on(upd_in, jac_in, pre_in, upd, jac, pre, upd_v, jac_v, pre_v, sem_in, sem_out):
    parts = [(upd_in, upd_v, upd), (pre_in, pre_v, pre)]
    for n in range(0, K, 4):
        part = pl.ds(n, 4)
        parts.append((jac_in.at[part], jac_v.at[part], jac.at[part]))
    reads = [pltpu.make_async_copy(src, mid, sem_in.at[n]) for n, (src, mid, _) in enumerate(parts)]
    writes = [pltpu.make_async_copy(mid, dst, sem_out.at[n]) for n, (_, mid, dst) in enumerate(parts)]
    for read in reads:
        read.start()
    for read, write in zip(reads, writes):
        read.wait()
        write.start()
    for write in writes:
        write.wait()


def local(stamps, stamp_target, pair_counts, conductance, block_cols, newton_residual):
    hbm = pl.BlockSpec(memory_space=pl.ANY)
    f32, i32 = jnp.float32, jnp.int32
    dma = pltpu.SemaphoreType.DMA
    shapes = (
            jax.ShapeDtypeStruct((8, NBR), f32),
            jax.ShapeDtypeStruct((K, 8, 8, NBR), f32),
            jax.ShapeDtypeStruct((8, NBR), f32),
    )
    results = pl.pallas_call(
        solver_kernel,
        out_shape=shapes,
        in_specs=[hbm] * 6,
        out_specs=(hbm, hbm, hbm),
        scratch_shapes=[
            pltpu.VMEM((DEVICES, LANES), i32),
            pltpu.VMEM((1, LANES), i32),
            pltpu.VMEM((8, NBR), f32),
            pltpu.VMEM((8, NBR), f32),
            pltpu.VMEM((K, NBR), i32),
            pltpu.VMEM((8, NBR), f32),
            pltpu.VMEM((16, 8, LANES), i32),
            pltpu.VMEM((16, 8, LANES), i32),
            pltpu.VMEM((16, 8, LANES), i32),
            pltpu.VMEM((16, 8, LANES), i32),
            pltpu.VMEM((NBLK, 1, LANES), f32),
            dma((2,)), dma((5,)), dma((2,)),
            pltpu.VMEM((DEVICES, 64, LANES), f32),
            pltpu.VMEM((DEVICES, 24, LANES), f32),
            pltpu.VMEM((DEVICES, 24, LANES), f32),
            pltpu.VMEM((DEVICES, LANES), f32),
            pltpu.VMEM((DEVICES, LANES), i32),
            pltpu.VMEM((64, LANES), f32),
            pltpu.VMEM((1, LANES), f32),
            pltpu.VMEM((1, LANES), f32),
            pltpu.VMEM((K, 8, 8, NBR), f32),
            pltpu.VMEM((8, 8, NBR), f32),
            dma((16,)), dma, dma((16,)), dma((4,)), dma,
            pltpu.VMEM((NBLK, 8, NBR), f32),
            pltpu.VMEM((NBLK, 8, NBR), f32),
            pltpu.VMEM((NBLK, 8, NBR), f32),
            pltpu.VMEM((DEVICES, LANES), f32),
            pltpu.VMEM((2, DEVICES, LANES), f32),
            pltpu.VMEM((DEVICES, LANES), i32),
            pltpu.VMEM((DEVICES, LANES), i32),
            pltpu.VMEM((1, LANES), f32),
            pltpu.VMEM((2, NGRP, 1, LANES), f32),
            pltpu.VMEM((1, LANES), f32),
            pltpu.VMEM((DEVICES, LANES), f32),
            pltpu.VMEM((KRYLOV + 1, 8, NBR), f32),
            pltpu.VMEM((KRYLOV, 8, NBR), f32),
            pltpu.VMEM((KRYLOV + 1, 8, LANES), f32),
            pltpu.VMEM((KRYLOV, 8, LANES), f32),
            pltpu.VMEM((8, NBR), i32),
            pltpu.VMEM((1, NBR), i32),
            dma, dma, dma, dma, dma((3,)), dma((5,)), dma((5,)), dma((5,)), dma((3, 3)), dma((3,)),
        ],
        compiler_params=pltpu.CompilerParams(collective_id=0, has_side_effects=True, vmem_limit_bytes=62 * 1024 * 1024),
    )(stamps, stamp_target.reshape(DEVICES, LANES), pair_counts, conductance, newton_residual, block_cols)
    return pl.pallas_call(
        hand_on,
        out_shape=shapes,
        in_specs=[hbm] * 3,
        out_specs=(hbm, hbm, hbm),
        scratch_shapes=[
            pltpu.VMEM((8, NBR), f32), pltpu.VMEM((K, 8, 8, NBR), f32), pltpu.VMEM((8, NBR), f32), dma((6,)), dma((6,)),
        ],
        compiler_params=pltpu.CompilerParams(vmem_limit_bytes=62 * 1024 * 1024),
    )(*results)


def solution(mesh):
    return jax.shard_map(
        local,
        mesh=mesh,
        in_specs=(
            P(AXES, None, None, None),
            P(AXES, None, None),
            P(AXES, None),
            P(None, AXES),
            P(None, AXES),
            P(None, AXES),
        ),
        out_specs=(P(None, AXES), P(None, None, None, AXES), P(None, AXES)),
        check_vma=False,
    )
```

```python
import functools
import jax
import jax.numpy as jnp
from jax import lax
from jax.experimental import pallas as pl
from jax.experimental.pallas import tpu as pltpu
from jax.sharding import PartitionSpec as P

K = 16
KRYLOV = 5
NBR = 256
NGRP = 8
NBLK = 16
DEVICES = 128
LANES = 128
FRONT = 32
EPS = 1e-06
MESH = pl.DeviceIdType.MESH
AXES = ("grp", "blk")


def bf(x):
    return x.astype(jnp.float32).astype(jnp.bfloat16)


def iota(shape, dim):
    return lax.broadcasted_iota(jnp.int32, shape, dim)


def lane_pick(table, index):
    return jnp.take_along_axis(table, index, axis=1, mode="promise_in_bounds")


def fold_rows(parts):
    row = iota(parts[0].shape, 0)
    step = 1
    while len(parts) > 1:
        even = (row & step) == 0
        merged = []
        for first, second in zip(parts[0::2], parts[1::2]):
            kept = jnp.where(even, first, second)
            moved = jnp.where(even, second, first)
            merged.append(kept + pltpu.roll(moved, step, 0))
        parts = merged
        step *= 2
    return parts[0]


def block_mul(blocks, vector):
    return fold_rows([blocks[a] * vector for a in range(8)])


def small_solve(gram, scales):
    inv = [1.0 / s for s in scales] + [1.0]
    sc = list(scales) + [1.0]
    n = KRYLOV + 1
    g = [[None] * n for _ in range(n)]
    for l in range(n):
        for m in range(l + 1):
            val = gram[l][m] * sc[l] * sc[m]
            g[l][m] = val
            g[m][l] = val
    beta = jnp.sqrt(gram[0][0] + EPS)
    basis = [[inv[0] / beta]]
    hess = []
    for j in range(KRYLOV):
        b = basis[j]
        w = [None] * (j + 2)
        for l in range(j + 1):
            w[l] = b[l] if w[l] is None else w[l] + b[l]
            w[l + 1] = b[l] * inv[l + 1]
        gw = []
        for l in range(j + 2):
            t = g[l][0] * w[0]
            for m in range(1, j + 2):
                t = t + g[l][m] * w[m]
            gw.append(t)
        column = []
        for i in range(j + 1):
            t = basis[i][0] * gw[0]
            for l in range(1, i + 1):
                t = t + basis[i][l] * gw[l]
            column.append(t)
        for i in range(j + 1):
            for l in range(i + 1):
                w[l] = w[l] - column[i] * basis[i][l]
        sq = None
        for l in range(j + 2):
            t = g[l][0] * w[0]
            for m in range(1, j + 2):
                t = t + g[l][m] * w[m]
            sq = t * w[l] if sq is None else sq + t * w[l]
        length = jnp.sqrt(jnp.maximum(sq, 0.0) + EPS)
        column.append(length)
        hess.append(column)
        scale = 1.0 / length
        basis.append([x * scale for x in w])
    work = [[None] * KRYLOV for _ in range(KRYLOV)]
    for p in range(KRYLOV):
        for q in range(p + 1):
            t = hess[p][0] * hess[q][0]
            for i in range(1, q + 2):
                t = t + hess[p][i] * hess[q][i]
            work[p][q] = t
            work[q][p] = t
    vec = [beta * hess[p][0] for p in range(KRYLOV)]
    for p in range(KRYLOV):
        scale = 1.0 / work[p][p]
        top = [x * scale for x in work[p]]
        tv = vec[p] * scale
        for q in range(KRYLOV):
            if q == p:
                continue
            f = work[q][p]
            work[q] = [x - f * y for x, y in zip(work[q], top)]
            vec[q] = vec[q] - f * tv
        work[p] = top
        vec[p] = tv
    out = []
    for l in range(KRYLOV):
        t = None
        for j in range(l, KRYLOV):
            x = vec[j] * basis[j][l]
            t = x if t is None else t + x
        out.append(t * sc[l])
    return out


def solver_kernel(stamps, target_in, counts_in, cond_in, res_in, cols_in, upd_out, jac_out, pre_out,
                  target, counts, cond, res, cols, upd, idx_lo, idx_hi, far_lo, far_hi, gbuf, sem_g, sem_i, sem_o,
                  stage, sbuf, rbuf_s, trep, cntb, tail, ttail, ttsrc, jac, dinv, sem_h, sem_ss, sem_rs, sem_t, sem_j,
                  buf_a, buf_b, buf_c, fsrc, fbuf, req_src, req, nsrc, nbuf, rsrc, rbuf,
                  us, ss, gp, sig, pidx, lst,
                  sem_sa, sem_sb, sem_sc, sem_sf, sem_sn, sem_ra, sem_rb, sem_rc, sem_rf, sem_rn):
    g, i = lax.axis_index("grp"), lax.axis_index("blk")
    me = g * NBLK + i

    def mate(o):
        return (g, (i + o) & (NBLK - 1))

    def peer(o):
        return ((g + o) & (NGRP - 1), i)

    def far_dev(t):
        return (g + 1 + t // NBLK) & (NGRP - 1), (i + t) & (NBLK - 1)

    barrier = pltpu.get_barrier_semaphore()

    def farthest_first(t):
        low = t & 37
        return me ^ (((low ^ 37) << 1) | (low ^ ((t >> 1) & 37)) | (~t & 16))

    def chunk_at(t):
        low = (t >> 2) & 1
        return my_chunk ^ (((low ^ 1) << 3) | ((low ^ (t >> 3)) << 2) | (~t & 3))

    def greet(t, c):
        d = farthest_first(t)
        pl.semaphore_signal(barrier, inc=1, device_id=(d // NBLK, d & (NBLK - 1)), device_id_type=MESH)
        return c

    lax.fori_loop(0, DEVICES - 1, greet, 0)

    my_chunk = me // 8

    def load(t):
        first = pl.multiple_of(((my_chunk + t) & 15) * 8, 8)
        return pltpu.make_async_copy(stamps.at[0, pl.ds(first, 8)], stage.at[pl.ds(first, 8)], sem_h.at[t])

    def start_load(t, c):
        load(t).start()
        return c

    reads = [
        pltpu.make_async_copy(src, dst, sem_i.at[n])
        for n, (src, dst) in enumerate(
            [(cols_in, cols), (target_in, target), (counts_in, counts), (cond_in, cond), (res_in, res)])
    ]
    for read in reads:
        read.start()
    lax.fori_loop(0, 16, start_load, 0)
    jac[...] = jnp.zeros_like(jac)
    us[...] = jnp.zeros_like(us)
    for read in reads:
        read.wait()
    us[0] = -res[...]

    nt = (((1,), (1,)), ((), ()))
    lane_big = iota((DEVICES, LANES), 1)
    row_big = iota((DEVICES, LANES), 0)
    count = jnp.sum(jnp.where(lane_big == row_big, counts[...], 0), axis=1, keepdims=True)
    count = jnp.broadcast_to(count, (DEVICES, LANES))
    cntb[...] = count
    tgt = jnp.where((lane_big < count) & (row_big != me), target[...], -1)
    trep[...] = lane_pick(tgt, lane_big & (FRONT - 1)).astype(jnp.float32)
    nxt = (me + 1) & (DEVICES - 1)
    lane1 = iota((1, LANES), 1)
    ttsrc[...] = jnp.where((lane1 >= FRONT) & (lane1 < cntb[pl.ds(nxt, 1), :]), target[pl.ds(nxt, 1), :], -1).astype(jnp.float32)
    own_target = jnp.where(lane1 < cntb[pl.ds(me, 1), :], target[pl.ds(me, 1), :], -1)
    quarter = lax.shift_right_logical(iota((16, LANES), 1), 5)

    def pack(t, c):
        load(t).wait()
        first = pl.multiple_of(((my_chunk + t) & 15) * 8, 8)
        rows = trep[pl.ds(first, 8), :]
        for e in range(8):
            x = stage[first + e, 0:16, :]
            for q in range(1, 4):
                x = jnp.where(quarter == q, pltpu.roll(stage[first + e, 16 * q : 16 * q + 16, :], 32 * q, 1), x)
            sbuf[first + e, 0:16, :] = x
            sbuf[first + e, 16:17, :] = rows[e : e + 1]
        return c

    lax.fori_loop(0, 16, pack, 0)
    rbuf_s[me] = sbuf[me]
    own_first = pl.multiple_of(my_chunk * 8, 8)
    pl.semaphore_wait(barrier, DEVICES - 1)

    tail_dev = (nxt // NBLK, nxt & (NBLK - 1))
    tail_copy = pltpu.make_async_remote_copy(
        src_ref=stage.at[nxt], dst_ref=tail, send_sem=sem_t.at[0], recv_sem=sem_t.at[1], device_id=tail_dev, device_id_type=MESH)
    tail_copy.start()
    ttail_copy = pltpu.make_async_remote_copy(
        src_ref=ttsrc, dst_ref=ttail, send_sem=sem_t.at[2], recv_sem=sem_t.at[3], device_id=tail_dev, device_id_type=MESH)
    ttail_copy.start()

    def stamp_copy(d):
        return pltpu.make_async_remote_copy(
            src_ref=sbuf.at[d, pl.ds(0, 17)], dst_ref=rbuf_s.at[me, pl.ds(0, 17)], send_sem=sem_ss, recv_sem=sem_rs.at[my_chunk],
            device_id=(d // NBLK, d & (NBLK - 1)), device_id_type=MESH)

    in_chunk = (6, 2, 7, 5, 1, 3, 4, 0)

    def send_chunk(t, c):
        first = chunk_at(t) * 8
        for e in in_chunk:
            stamp_copy(first + ((me ^ e) & 7)).start()
        return c

    lax.fori_loop(0, 15, send_chunk, 0)
    for e in in_chunk[:7]:
        stamp_copy(own_first + ((me ^ e) & 7)).start()

    owner_row = iota((DEVICES, NBR), 0)
    upper = bf(iota((NBR, NBR), 0) < iota((NBR, NBR), 1))
    before = jnp.zeros((DEVICES, 1), jnp.float32)
    wanted = jnp.zeros((DEVICES, LANES), jnp.float32)
    listed = jnp.zeros((8, NBR), jnp.float32)
    nt = (((1,), (1,)), ((), ()))
    for k in range(8):
        col = cols[8 + k : 9 + k, :]
        owner = lax.shift_right_logical(col, 8)
        row = col & 255
        hit = owner_row == owner
        one = jnp.where(hit, 1.0, 0.0)
        ahead = jnp.dot(one.astype(jnp.bfloat16), upper, preferred_element_type=jnp.float32) + before
        rank = jnp.sum(jnp.where(hit, ahead, 0.0), axis=0, keepdims=True).astype(jnp.int32)
        before = before + jnp.sum(one, axis=1, keepdims=True)
        place = owner * 16 + rank
        pidx[k : k + 1, :] = place
        rowf = row.astype(jnp.float32)
        ranked = jnp.where((owner_row & 15) == rank, rowf, 0.0).astype(jnp.bfloat16)
        wanted = wanted + lax.dot_general(one.astype(jnp.bfloat16), ranked, nt, preferred_element_type=jnp.float32)
        mine = bf(iota((NBR, NBR), 0) == place - g * NBR)
        rows8 = jnp.broadcast_to(rowf, (8, NBR)).astype(jnp.bfloat16)
        listed = listed + lax.dot_general(rows8, mine, nt, preferred_element_type=jnp.float32)
    req_src[...] = wanted.astype(jnp.int32)
    lst[...] = (lax.shift_right_logical(iota((8, NBR), 1), 4) * NBR + listed.astype(jnp.int32))[0:1]

    for q in range(16):
        half = slice(q % 2 * LANES, (q % 2 + 1) * LANES)
        if q < 14:
            idx = cols[1 + q // 2 : 2 + q // 2, half] - g * (NBLK * NBR)
        else:
            idx = lst[:, half]
        idx = jnp.broadcast_to(idx, (8, LANES))
        idx_lo[q] = idx & 127
        idx_hi[q] = lax.shift_right_logical(idx, 7)
        idx = jnp.broadcast_to(pidx[q // 2 : q // 2 + 1, half], (8, LANES))
        far_lo[q] = idx & 127
        far_hi[q] = lax.shift_right_logical(idx, 7)

    def ask(t, c):
        dg, di = far_dev(t)
        d = dg * NBLK + di
        pltpu.make_async_remote_copy(
            src_ref=req_src.at[pl.ds(d, 1)], dst_ref=req.at[pl.ds(me, 1)], send_sem=sem_sn.at[2], recv_sem=sem_rn.at[2],
            device_id=(dg, di), device_id_type=MESH).start()
        return c

    lax.fori_loop(0, 112, ask, 0)
    rsrc[...] = jnp.zeros_like(rsrc)

    def whole(ref, rows, send, recv):
        return pltpu.make_async_remote_copy(
            src_ref=ref.at[pl.ds(0, rows)], dst_ref=ref.at[pl.ds(0, rows)], send_sem=send, recv_sem=recv,
            device_id=mate(1), device_id_type=MESH)

    node = iota((NBR, NBR), 0)

    def add_slots(values, goal):
        slot_k = lax.shift_right_arithmetic(goal, 8)
        values = jnp.where(goal >= 0, values, 0.0)
        high = values.astype(jnp.bfloat16)
        low = (values - high.astype(jnp.float32)).astype(jnp.bfloat16)
        both = jnp.concatenate([high, low], axis=1)
        there = bf(node == (goal & 255))
        there = jnp.concatenate([there, there], axis=1)
        twice = jnp.concatenate([slot_k, slot_k], axis=1)
        for k0 in range(0, K, 4):
            rows = [both * bf(jnp.broadcast_to(twice == k0 + k, (64, 2 * NBR))) for k in range(4)]
            part = lax.dot_general(jnp.concatenate(rows, axis=0), there, nt, preferred_element_type=jnp.float32)
            jac[k0 : k0 + 4] = jac[k0 : k0 + 4] + part.reshape(4, 8, 8, NBR)

    def add_chunk(first):
        wide, goals = [], []
        for tile in range(2):
            blocks = [rbuf_s[first + 4 * tile + s, 0:16, :] for s in range(4)]
            parts = []
            for q in range(4):
                x = None
                for s in range(4):
                    y = blocks[s] if s == q else pltpu.roll(blocks[s], (s - q) * 32 % LANES, 1)
                    x = y if x is None else jnp.where(quarter == s, y, x)
                parts.append(x)
            wide.append(jnp.concatenate(parts, axis=0))
            x = rbuf_s[first + 4 * tile, 16:17, :]
            for s in range(1, 4):
                x = jnp.where(quarter[0:1] == s, rbuf_s[first + 4 * tile + s, 16:17, :], x)
            goals.append(x.astype(jnp.int32))
        add_slots(jnp.concatenate(wide, axis=1), jnp.concatenate(goals, axis=1))

    def chunk_wait(first, count, sem):
        return pltpu.make_async_remote_copy(
            src_ref=sbuf.at[pl.ds(0, count), pl.ds(0, 17)], dst_ref=rbuf_s.at[pl.ds(0, count), pl.ds(0, 17)],
            send_sem=sem_ss, recv_sem=sem, device_id=mate(1), device_id_type=MESH)

    tail_copy.wait_recv()
    ttail_copy.wait_recv()
    add_slots(
        jnp.concatenate([stage[me], tail[...]], axis=1),
        jnp.concatenate([own_target, ttail[...].astype(jnp.int32)], axis=1))
    def take_chunk(t, c):
        chunk = chunk_at(t)
        first = pl.multiple_of(chunk * 8, 8)
        chunk_wait(first, 8, sem_rs.at[chunk]).wait_recv()
        add_chunk(first)
        return c

    lax.fori_loop(0, 15, take_chunk, 0)
    chunk_wait(own_first, 7, sem_rs.at[my_chunk]).wait_recv()
    add_chunk(own_first)
    sub8 = iota((8, NBR), 0)
    for a in range(8):
        jac[0, a] = jac[0, a] + jnp.where(sub8 == a, jnp.broadcast_to(cond[a : a + 1, :], (8, NBR)), 0.0)
    jac_copy = pltpu.make_async_copy(jac, jac_out, sem_j)
    jac_copy.start()

    work = [jac[0, a] for a in range(8)]
    inverse = [jnp.where(sub8 == a, 1.0, 0.0) for a in range(8)]
    for p in range(8):
        scale = 1.0 / work[p][p : p + 1, :]
        top_w, top_i = work[p] * scale, inverse[p] * scale
        for a in range(8):
            if a != p:
                factor = work[a][p : p + 1, :]
                work[a] = work[a] - factor * top_w
                inverse[a] = inverse[a] - factor * top_i
        work[p], inverse[p] = top_w, top_i
    for a in range(8):
        dinv[a] = inverse[a]
    chunk_wait(own_first, 127, sem_ss).wait_send()
    tail_copy.wait_send()
    ttail_copy.wait_send()
    asked = whole(req, 112, sem_sn.at[2], sem_rn.at[2])
    asked.wait_recv()
    asked.wait_send()

    y, z_at = i // 4, i & 3
    by_hops = [[] for _ in range(5)]
    for oy in range(4):
        for oz in range(4):
            by_hops[min(oy, 4 - oy) + min(oz, 4 - oz)].append((oy, oz))

    def spread(buf, send, recv):
        for hops in (4, 3, 2, 1):
            for oy, oz in by_hops[hops]:
                to = ((y + oy) & 3) * 4 + ((z_at + oz) & 3)
                pltpu.make_async_remote_copy(
                    src_ref=buf.at[i], dst_ref=buf.at[i], send_sem=send, recv_sem=recv.at[hops],
                    device_id=(g, to), device_id_type=MESH).start()

    def sent(buf, send, recv):
        whole(buf, 15, send, recv.at[0]).wait_send()

    def near_pick(buf, send, recv):
        acc = [jnp.zeros((8, LANES), jnp.float32)] * 16
        for part in ((0, 1, 2, 3), (4,)):
            tables = []
            for hops in part:
                if hops:
                    whole(buf, len(by_hops[hops]), send, recv.at[hops]).wait_recv()
                for oy, oz in by_hops[hops]:
                    tables.append(((y - oy) & 3) * 4 + ((z_at - oz) & 3))
            for q in range(16):
                lo, hi, x = idx_lo[q], idx_hi[q], acc[q]
                for s in tables:
                    for h in range(2):
                        x = jnp.where(hi == 2 * s + h, lane_pick(buf[s, :, h * LANES : (h + 1) * LANES], lo), x)
                acc[q] = x
        return acc

    def add_slot(acc, k, picked):
        return [x + jac[k, a] * picked for a, x in enumerate(acc)]

    def joined(first, second):
        return jnp.concatenate([first, second], axis=1)

    def near_couple(buf, send, recv):
        picked = near_pick(buf, send, recv)
        acc = [jnp.zeros((8, NBR), jnp.float32)] * 8
        for k in range(7):
            acc = add_slot(acc, 1 + k, joined(picked[2 * k], picked[2 * k + 1]))
        for k in range(8):
            got = []
            for h in range(2):
                x = jnp.zeros((8, LANES), jnp.float32)
                for v in range(2):
                    x = jnp.where(far_hi[2 * k + h] == 2 * g + v, lane_pick(picked[14 + v], far_lo[2 * k + h]), x)
                got.append(x)
            acc = add_slot(acc, 8 + k, joined(*got))
        return fold_rows(acc)

    lane16 = iota((8, LANES), 1) & 15
    lane_group = lax.shift_right_logical(iota((8, LANES), 1), 4)
    turn = iota((8, LANES), 0) * 16 + lane16
    x_at, core = g // 2, g & 1
    far_groups = [[(0, 1)], [(1, 0), (1, 1), (3, 0), (3, 1)], [(2, 0), (2, 1)]]

    def step(j, carry):
        slot = j & 1
        u = us[j]
        z = block_mul(dinv, u)
        buf_a[i] = z
        spread(buf_a, sem_sa, sem_ra)
        sq = u * u
        gbuf[i] = jnp.sum(sq[:, :LANES] + sq[:, LANES:], axis=0, keepdims=True)
        for o in range(1, NBLK):
            pltpu.make_async_remote_copy(
                src_ref=gbuf.at[i], dst_ref=gbuf.at[i], send_sem=sem_g.at[0], recv_sem=sem_g.at[1],
                device_id=mate(o), device_id_type=MESH).start()
        dots = []
        for l in range(6):
            t = u * us[l]
            dots.append(t[:, :LANES] + t[:, LANES:])
        zero = jnp.zeros((8, LANES), jnp.float32)
        gp[j] = fold_rows(dots + [zero, zero])
        z = block_mul(dinv, u - near_couple(buf_a, sem_sa, sem_ra))
        buf_b[i] = z
        spread(buf_b, sem_sb, sem_rb)
        done_g = whole(gbuf, 15, sem_g.at[0], sem_g.at[1])
        done_g.wait_recv()
        nrow = gbuf[0]
        for s in range(1, NBLK):
            nrow = nrow + gbuf[s]
        nsrc[...] = nrow
        for o in range(1, NGRP):
            pltpu.make_async_remote_copy(
                src_ref=nsrc, dst_ref=nbuf.at[slot, g], send_sem=sem_sn.at[slot], recv_sem=sem_rn.at[slot],
                device_id=peer(o), device_id_type=MESH).start()
        nbuf[slot, g] = nrow
        done_g.wait_send()
        sent(buf_a, sem_sa, sem_ra)
        z = block_mul(dinv, u - near_couple(buf_b, sem_sb, sem_rb))
        buf_c[i] = z

        def far_send(dx, dc, half):
            dg = ((x_at + dx) & 3) * 2 + (core ^ dc)
            first = pl.multiple_of(dg * NBLK + half * 8, 8)
            idx = req[pl.ds(first, 8), :]
            lo, hi = idx & 127, lax.shift_right_logical(idx, 7)
            out = jnp.zeros((8, LANES), jnp.float32)
            for b in range(8):
                for h in range(2):
                    table = jnp.broadcast_to(z[b : b + 1, h * LANES : (h + 1) * LANES], (8, LANES))
                    out = jnp.where((hi == h) & (lane_group == b), lane_pick(table, lo), out)
            fsrc[pl.ds(first, 8), :] = out
            for d in range(8):
                pltpu.make_async_remote_copy(
                    src_ref=fsrc.at[pl.ds(first + d, 1)], dst_ref=fbuf.at[slot, pl.ds(me, 1)],
                    send_sem=sem_sf, recv_sem=sem_rf.at[slot, {0: 0, 1: 1, 3: 1, 2: 2}[dx]],
                    device_id=(dg, half * 8 + d), device_id_type=MESH).start()

        for dx, dc in far_groups[2]:
            for half in range(2):
                far_send(dx, dc, half)
        spread(buf_c, sem_sc, sem_rc)
        for dx, dc in far_groups[1] + far_groups[0]:
            for half in range(2):
                far_send(dx, dc, half)
        sent(buf_b, sem_sb, sem_rb)
        ss[j] = z
        acc = [jac[0, a] * z for a in range(8)]
        picked = near_pick(buf_c, sem_sc, sem_rc)
        for k in range(7):
            acc = add_slot(acc, 1 + k, joined(picked[2 * k], picked[2 * k + 1]))
        got = [jnp.zeros((8, LANES), jnp.float32)] * 16

        def place_far(tables):
            for q in range(16):
                lo, hi, x = far_lo[q], far_hi[q], got[q]
                for at, table in tables:
                    x = jnp.where(hi == at, lane_pick(table, lo), x)
                got[q] = x

        place_far([(2 * g + v, picked[14 + v]) for v in range(2)])
        sent(buf_c, sem_sc, sem_rc)

        def far_part(count, cls):
            return pltpu.make_async_remote_copy(
                src_ref=fsrc.at[pl.ds(0, count)], dst_ref=fbuf.at[slot, pl.ds(0, count)], send_sem=sem_sf,
                recv_sem=sem_rf.at[slot, cls], device_id=mate(1), device_id_type=MESH)

        done_n = pltpu.make_async_remote_copy(
            src_ref=nbuf.at[slot, pl.ds(0, 7)], dst_ref=nbuf.at[slot, pl.ds(0, 7)], send_sem=sem_sn.at[slot], recv_sem=sem_rn.at[slot],
            device_id=mate(1), device_id_type=MESH)
        done_n.wait_recv()
        total = nbuf[slot, 0]
        for s in range(1, NGRP):
            total = total + nbuf[slot, s]
        scale = lax.rsqrt(jnp.maximum(jnp.sum(total, axis=1, keepdims=True), 1e-12))
        sig[j] = jnp.broadcast_to(scale, (8, LANES))
        for cls, groups in enumerate(far_groups):
            far_part(16 * len(groups), cls).wait_recv()
            tables = []
            for dx, dc in groups:
                dg = ((x_at + dx) & 3) * 2 + (core ^ dc)
                for half in range(2):
                    rows = fbuf[slot, pl.ds(pl.multiple_of(dg * NBLK + half * 8, 8), 8), :]
                    table = jnp.zeros((8, LANES), jnp.float32)
                    for o in range(8):
                        table = jnp.where(lane_group == o, lane_pick(jnp.broadcast_to(rows[o : o + 1], (8, LANES)), turn), table)
                    tables.append((2 * dg + half, table))
            place_far(tables)
        for k in range(8):
            acc = add_slot(acc, 8 + k, joined(got[2 * k], got[2 * k + 1]))
        image = fold_rows(acc)
        us[j + 1] = (image - u) * scale
        done_n.wait_send()
        far_part(112, 0).wait_send()
        return carry

    lax.fori_loop(0, KRYLOV, step, 0)

    pre_copy = pltpu.make_async_copy(ss.at[0], pre_out, sem_o.at[0])
    pre_copy.start()
    u = us[KRYLOV]
    dots = []
    for l in range(6):
        t = u * us[l]
        dots.append(t[:, :LANES] + t[:, LANES:])
    zero = jnp.zeros((8, LANES), jnp.float32)
    gp[KRYLOV] = fold_rows(dots + [zero, zero])
    row = jnp.zeros((1, LANES), jnp.float32)
    lane = iota((8, LANES), 1)
    sub = iota((8, LANES), 0)
    for j in range(6):
        s = jnp.sum(gp[j], axis=1, keepdims=True)
        row = row + jnp.sum(jnp.where(lane == 8 * j + sub, s, 0.0), axis=0, keepdims=True)
    rsrc[...] = row

    def tell(t, c):
        d = farthest_first(t)
        pltpu.make_async_remote_copy(
            src_ref=rsrc, dst_ref=rbuf.at[pl.ds(me, 1)], send_sem=sem_sf, recv_sem=sem_rf.at[2, 0],
            device_id=(d // NBLK, d & (NBLK - 1)), device_id_type=MESH).start()
        return c

    lax.fori_loop(0, DEVICES - 1, tell, 0)
    rbuf[pl.ds(me, 1), :] = row
    done = whole(rbuf, 127, sem_sf, sem_rf.at[2, 0])
    done.wait_recv()
    done.wait_send()
    total = rbuf[0:8, :]
    for q in range(1, 16):
        total = total + rbuf[8 * q : 8 * q + 8, :]
    total = jnp.sum(total, axis=0, keepdims=True)
    gram = [[jnp.broadcast_to(total[:, 8 * j + l : 8 * j + l + 1], (8, LANES)) for l in range(j + 1)] for j in range(6)]
    weights = small_solve(gram, [sig[j] for j in range(KRYLOV)])
    for h in range(2):
        part = slice(h * LANES, (h + 1) * LANES)
        x = weights[0] * ss[0, :, part]
        for l in range(1, KRYLOV):
            x = x + weights[l] * ss[l, :, part]
        upd[:, part] = x
    upd_copy = pltpu.make_async_copy(upd, upd_out, sem_o.at[1])
    upd_copy.start()
    jac_copy.wait()
    pre_copy.wait()
    upd_copy.wait()


def hand_on(upd_in, jac_in, pre_in, upd, jac, pre, upd_v, jac_v, pre_v, sem_in, sem_out):
    parts = [(upd_in, upd_v, upd), (pre_in, pre_v, pre)]
    for n in range(0, K, 4):
        part = pl.ds(n, 4)
        parts.append((jac_in.at[part], jac_v.at[part], jac.at[part]))
    reads = [pltpu.make_async_copy(src, mid, sem_in.at[n]) for n, (src, mid, _) in enumerate(parts)]
    writes = [pltpu.make_async_copy(mid, dst, sem_out.at[n]) for n, (_, mid, dst) in enumerate(parts)]
    for read in reads:
        read.start()
    for read, write in zip(reads, writes):
        read.wait()
        write.start()
    for write in writes:
        write.wait()


def local(stamps, stamp_target, pair_counts, conductance, block_cols, newton_residual):
    hbm = pl.BlockSpec(memory_space=pl.ANY)
    f32, i32 = jnp.float32, jnp.int32
    dma = pltpu.SemaphoreType.DMA
    shapes = (
            jax.ShapeDtypeStruct((8, NBR), f32),
            jax.ShapeDtypeStruct((K, 8, 8, NBR), f32),
            jax.ShapeDtypeStruct((8, NBR), f32),
    )
    results = pl.pallas_call(
        solver_kernel,
        out_shape=shapes,
        in_specs=[hbm] * 6,
        out_specs=(hbm, hbm, hbm),
        scratch_shapes=[
            pltpu.VMEM((DEVICES, LANES), i32),
            pltpu.VMEM((1, LANES), i32),
            pltpu.VMEM((8, NBR), f32),
            pltpu.VMEM((8, NBR), f32),
            pltpu.VMEM((K, NBR), i32),
            pltpu.VMEM((8, NBR), f32),
            pltpu.VMEM((16, 8, LANES), i32),
            pltpu.VMEM((16, 8, LANES), i32),
            pltpu.VMEM((16, 8, LANES), i32),
            pltpu.VMEM((16, 8, LANES), i32),
            pltpu.VMEM((NBLK, 1, LANES), f32),
            dma((2,)), dma((5,)), dma((2,)),
            pltpu.VMEM((DEVICES, 64, LANES), f32),
            pltpu.VMEM((DEVICES, 24, LANES), f32),
            pltpu.VMEM((DEVICES, 24, LANES), f32),
            pltpu.VMEM((DEVICES, LANES), f32),
            pltpu.VMEM((DEVICES, LANES), i32),
            pltpu.VMEM((64, LANES), f32),
            pltpu.VMEM((1, LANES), f32),
            pltpu.VMEM((1, LANES), f32),
            pltpu.VMEM((K, 8, 8, NBR), f32),
            pltpu.VMEM((8, 8, NBR), f32),
            dma((16,)), dma, dma((16,)), dma((4,)), dma,
            pltpu.VMEM((NBLK, 8, NBR), f32),
            pltpu.VMEM((NBLK, 8, NBR), f32),
            pltpu.VMEM((NBLK, 8, NBR), f32),
            pltpu.VMEM((DEVICES, LANES), f32),
            pltpu.VMEM((2, DEVICES, LANES), f32),
            pltpu.VMEM((DEVICES, LANES), i32),
            pltpu.VMEM((DEVICES, LANES), i32),
            pltpu.VMEM((1, LANES), f32),
            pltpu.VMEM((2, NGRP, 1, LANES), f32),
            pltpu.VMEM((1, LANES), f32),
            pltpu.VMEM((DEVICES, LANES), f32),
            pltpu.VMEM((KRYLOV + 1, 8, NBR), f32),
            pltpu.VMEM((KRYLOV, 8, NBR), f32),
            pltpu.VMEM((KRYLOV + 1, 8, LANES), f32),
            pltpu.VMEM((KRYLOV, 8, LANES), f32),
            pltpu.VMEM((8, NBR), i32),
            pltpu.VMEM((1, NBR), i32),
            dma, dma, dma, dma, dma((3,)), dma((5,)), dma((5,)), dma((5,)), dma((3, 3)), dma((3,)),
        ],
        compiler_params=pltpu.CompilerParams(collective_id=0, has_side_effects=True, vmem_limit_bytes=62 * 1024 * 1024),
    )(stamps, stamp_target.reshape(DEVICES, LANES), pair_counts, conductance, newton_residual, block_cols)
    return pl.pallas_call(
        hand_on,
        out_shape=shapes,
        in_specs=[hbm] * 3,
        out_specs=(hbm, hbm, hbm),
        scratch_shapes=[
            pltpu.VMEM((8, NBR), f32), pltpu.VMEM((K, 8, 8, NBR), f32), pltpu.VMEM((8, NBR), f32), dma((6,)), dma((6,)),
        ],
        compiler_params=pltpu.CompilerParams(vmem_limit_bytes=62 * 1024 * 1024),
    )(*results)


def solution(mesh):
    return jax.shard_map(
        local,
        mesh=mesh,
        in_specs=(
            P(AXES, None, None, None),
            P(AXES, None, None),
            P(AXES, None),
            P(None, AXES),
            P(None, AXES),
            P(None, AXES),
        ),
        out_specs=(P(None, AXES), P(None, None, None, AXES), P(None, AXES)),
        check_vma=False,
    )
```
